512 devices in a mesh: gx: 32 (over z_hi, y, core), gy: 16 (over x, z_lo).
Axes of the slice: x: 4, y: 4, z: 16 (z_hi: 4, z_lo: 4; z = z_hi * 4 + z_lo), core: 2. Of those that a mesh axis runs over, the one named last changes fastest.
Arguments:
- node_state: bfloat16 [262144, 256], P(('gx', 'gy')), may hold values from -6 to 6
- node_grad: bfloat16 [262144, 256], P(('gx', 'gy')), may hold values from -6 to 6
- edge_blocks: bfloat16 [2048, 3, 128, 128], P(('gx', 'gy')), may hold values from -0.3125 to 0.3125
- adjacency: int32 [2048, 3], P(('gx', 'gy')), may hold values from 0 to 3
- cut_source: int32 [32, 16, 4, 2], P('gx', 'gy'), may hold values from 0 to 3
- cut_target: int32 [32, 16, 4, 2], P('gx', 'gy'), may hold values from 0 to 3
- cut_blocks: bfloat16 [32, 16, 4, 2, 128, 128], P('gx', 'gy'), may hold values from -0.3125 to 0.3125
- clusters: int32 [262144], P(('gx', 'gy')), may hold values from 0 to 767, as said below
- edge_lift: bfloat16 [256, 256], replicated, may hold values from -0.375 to 0.375
- edge_bias: bfloat16 [256], replicated, may hold values from -3 to 3
- edge_emit: bfloat16 [256, 256], replicated, may hold values from -0.375 to 0.375
- node_lift: bfloat16 [768, 256], replicated, may hold values from -0.21875 to 0.21875
- node_bias: bfloat16 [256], replicated, may hold values from -3 to 3
- node_emit: bfloat16 [256, 256], replicated, may hold values from -0.375 to 0.375
- norm_gain: bfloat16 [256], replicated, may hold values from 0.5 to 1.5
Outputs:
- updated: bfloat16 [262144, 256], P(('gx', 'gy'))
- state_grad: bfloat16 [262144, 256], P(('gx', 'gy'))
- edgelift_grad: float32 [256, 256], replicated
- edgebias_grad: float32 [256], replicated
- edgeemit_grad: float32 [256, 256], replicated
- nodelift_grad: float32 [768, 256], replicated
- nodebias_grad: float32 [256], replicated
- nodeemit_grad: float32 [256, 256], replicated
- normgain_grad: float32 [256], replicated
The draws below stay inside these ranges and needn't reach their ends.
Inputs may be any that keep to these rules, and one draw needn't show every extreme that they name: `clusters`: clusters are numbered within a group (the same index along gy); cluster c is owned by the partition at index c // 24 along gx, and in every group each cluster is named by at least one node of its owner.
All inputs are finite; a program needn't handle non-finite values.
Results may differ from the reference program's by a relative error of at most 0.02.
Values may be sent and summed in bfloat16 or wider, within the bound.
No kernel may reach another device: no remote copies, remote signals or barrier semaphores. Data moves between devices by JAX's collectives and lax.ppermute only.
A program may use at most 64 MiB of HBM per device.

```python
import jax
import jax.numpy as jnp
from jax import lax

D = 256
HID = 256
TILE = 128
K = 3
CUT = 2
TILES_DEV = 4
CLUS_DEV = 24
NODE_DEV = 512
NODES = 262144
TILES = 2048
N_GX = 32
N_GY = 16


def draw_clusters(key, part):
    key = jax.random.fold_in(key, 7)
    key_perm, key_move, key_side, key_slot = jax.random.split(key, 4)
    partitions = N_GX * N_GY
    orders = jax.vmap(lambda subkey: jax.random.permutation(subkey, NODE_DEV))(jax.random.split(key_perm, partitions))
    orders = orders.reshape(N_GX, N_GY, NODE_DEV).astype(jnp.int32)
    position = jnp.arange(N_GX, dtype=jnp.int32)[:, None, None]
    opposite = (position + N_GX // 2) % N_GX
    anywhere = jax.random.randint(key_side, orders.shape, 0, N_GX)
    across = jax.random.randint(key_move, orders.shape, 0, 4) != 0
    target_part = jnp.where(across, opposite, anywhere)
    slotted = jax.random.randint(key_slot, orders.shape, 0, CLUS_DEV)
    chosen = jnp.where(orders < CLUS_DEV, position * CLUS_DEV + orders, target_part * CLUS_DEV + slotted)
    return chosen.reshape(-1).astype(jnp.int32)


def plant(entries, rng, low, largest):
    place = [jax.random.randint(jax.random.fold_in(rng, axis), (), 0, length) for axis, length in enumerate(entries.shape)]
    longest = entries.shape.index(max(entries.shape))
    neighbour = place[:longest] + [(place[longest] + 1) % entries.shape[longest]] + place[longest + 1:]
    return entries.at[tuple(place)].set(low).at[tuple(neighbour)].set(largest)


def shard_levels(stream_key, dims, pieces, smallest, largest):
    def one(dim, blocks):
        draws = jax.random.uniform(jax.random.fold_in(jax.random.fold_in(stream_key, 6), dim), (blocks,), jnp.float32, smallest / len(pieces), largest / len(pieces))
        return jnp.repeat(jnp.exp(draws), dims[dim] // blocks).reshape((-1,) + (1,) * (len(dims) - dim - 1))

    factor_of = one(*pieces[0])
    for cut in pieces[1:]:
        factor_of = factor_of * one(*cut)
    return factor_of


def noise(key, dims, scale, bound, cuts=(), kind=jnp.bfloat16):
    entries = jax.random.normal(key, dims, jnp.float32) * scale
    if len(cuts) > 0:
        entries = shard_levels(key, dims, cuts, -0.22, 0.18) * entries
    return jnp.clip(entries, min=-bound, max=bound).astype(kind)


def setup_inputs(seed: int = 0) -> dict:
    key_of = jax.random.split(jax.random.key(seed), 16)
    node_state = noise(key_of[0], (NODES, D), 1.0, 6.0, ((0, 512),))
    node_grad = noise(key_of[1], (NODES, D), 1.0, 6.0, ((0, 512),))
    edge_blocks = noise(key_of[2], (TILES, K, TILE, TILE), (K * TILE) ** -0.5, 0.3125, ((0, 512),))
    adjacency = plant(jax.random.randint(key_of[3], (TILES, K), 0, TILES_DEV), jax.random.fold_in(key_of[3], 1), 0, TILES_DEV - 1).astype(jnp.int32)
    cut_source = plant(jax.random.randint(key_of[4], (N_GX, N_GY, 4, CUT), 0, TILES_DEV), jax.random.fold_in(key_of[4], 1), 0, TILES_DEV - 1).astype(jnp.int32)
    cut_target = plant(jax.random.randint(key_of[5], (N_GX, N_GY, 4, CUT), 0, TILES_DEV), jax.random.fold_in(key_of[5], 1), 0, TILES_DEV - 1).astype(jnp.int32)
    cut_blocks = noise(key_of[6], (N_GX, N_GY, 4, CUT, TILE, TILE), (K * TILE) ** -0.5, 0.3125, ((0, 32), (1, 16)))
    clusters = draw_clusters(jax.random.fold_in(key_of[15], 71), 0)
    edge_lift = noise(key_of[8], (D, HID), D ** -0.5, 0.375)
    edge_bias = noise(key_of[9], (HID,), 0.5, 3.0)
    edge_emit = noise(key_of[10], (HID, D), HID ** -0.5, 0.375)
    node_lift = noise(key_of[11], (3 * D, HID), (3 * D) ** -0.5, 0.21875)
    node_bias = noise(key_of[12], (HID,), 0.5, 3.0)
    node_emit = noise(key_of[13], (HID, D), HID ** -0.5, 0.375)
    norm_gain = jnp.clip(1.0 + 0.1 * jax.random.normal(key_of[14], (D,), jnp.float32), 0.5, 1.5).astype(jnp.bfloat16)
    return {"node_state": node_state, "node_grad": node_grad, "edge_blocks": edge_blocks, "adjacency": adjacency, "cut_source": cut_source, "cut_target": cut_target, "cut_blocks": cut_blocks, "clusters": clusters, "edge_lift": edge_lift, "edge_bias": edge_bias, "edge_emit": edge_emit, "node_lift": node_lift, "node_bias": node_bias, "node_emit": node_emit, "norm_gain": norm_gain}


NORM_EPS = 1e-05
HIGHEST = lax.Precision.HIGHEST

def product(left, right):
    return jnp.dot(left, right, preferred_element_type=jnp.float32, precision=HIGHEST)

def product_across(left, right):
    return lax.dot_general(left, right, (((0,), (0,)), ((), ())), preferred_element_type=jnp.float32, precision=HIGHEST)

def product_back(left, right):
    return lax.dot_general(left, right, (((1,), (1,)), ((), ())), preferred_element_type=jnp.float32, precision=HIGHEST)

def silu_slope(operand):
    sigmoid = jax.nn.sigmoid(operand)
    return sigmoid * (1.0 + operand * (1.0 - sigmoid))

def edge_front(states, edge_lift, edge_bias):
    lifted = (product(states, edge_lift) + edge_bias.astype(jnp.float32)).astype(jnp.bfloat16)
    active = jax.nn.silu(lifted.astype(jnp.float32)).astype(jnp.bfloat16)
    return (lifted, active)

def cluster_mean(values, groups):
    segment_total = CLUS_DEV * N_GX
    partial_sums = jax.ops.segment_sum(values.astype(jnp.float32), groups, num_segments=segment_total)
    counts = jax.ops.segment_sum(jnp.ones(groups.shape, jnp.float32), groups, num_segments=segment_total)
    cluster_means = (partial_sums / counts[:, None]).astype(jnp.bfloat16)
    return cluster_means[groups]

def displace(values, axis_pos, offset):
    length = values.shape[axis_pos]
    padding = [(0, 0)] * values.ndim
    if offset > 0:
        padding[axis_pos] = (1, 0)
        return jnp.pad(lax.slice_in_dim(values, 0, length - 1, axis=axis_pos), padding)
    padding[axis_pos] = (0, 1)
    return jnp.pad(lax.slice_in_dim(values, 1, length, axis=axis_pos), padding)

def travel(partials, direction):
    received = [displace(partials[:, :, 0], 1, direction), displace(partials[:, :, 1], 1, -direction), displace(partials[:, :, 2], 0, direction), displace(partials[:, :, 3], 0, -direction)]
    return jnp.stack(received, axis=2)

def by_column(values, inner_shape):
    return jnp.swapaxes(values.reshape((N_GX, N_GY) + inner_shape), 0, 1)

def reference(node_state, node_grad, edge_blocks, adjacency, cut_source, cut_target, cut_blocks, clusters, edge_lift, edge_bias, edge_emit, node_lift, node_bias, node_emit, norm_gain):
    states = by_column(node_state, (NODE_DEV, D))
    upstream_all = by_column(node_grad, (NODE_DEV, D))
    blocks = by_column(edge_blocks, (TILES_DEV, K, TILE, TILE))
    neighbours = by_column(adjacency, (TILES_DEV, K))
    groups_all = by_column(clusters, (NODE_DEV,))
    sources = jnp.swapaxes(cut_source, 0, 1)
    targets = jnp.swapaxes(cut_target, 0, 1)
    cut_all = jnp.swapaxes(cut_blocks, 0, 1)
    tile_ids = jnp.arange(TILES_DEV, dtype=jnp.int32)
    lift_state = node_lift[:D]
    lift_agg = node_lift[D:2 * D]
    lift_coarse = node_lift[2 * D:]

    def front_device(state_dev, cut_dev, source_dev):
        lifted, active = edge_front(state_dev, edge_lift, edge_bias)
        message = product(active, edge_emit).astype(jnp.bfloat16)
        tiles_msg = message.reshape(TILES_DEV, TILE, D)
        partials = jnp.einsum('pcij,pcjf->pcif', cut_dev.astype(jnp.float32), tiles_msg[source_dev].astype(jnp.float32), precision=HIGHEST)
        return (tiles_msg, partials.astype(jnp.bfloat16))

    def front_column(inputs):
        return jax.vmap(front_device)(inputs[0], inputs[1], inputs[2])
    tiles_all, partials_all = lax.map(front_column, (states, cut_all, sources))
    arrived_all = travel(partials_all, 1)

    def aggregate_device(tiles_msg, arrived, block_dev, adjacency_dev, target_dev):
        local_sum = jnp.einsum('tkij,tkjf->tif', block_dev.astype(jnp.float32), tiles_msg[adjacency_dev].astype(jnp.float32), precision=HIGHEST)
        target_hot = (target_dev[:, :, None] == tile_ids).astype(jnp.float32)
        incoming = jnp.einsum('pct,pcif->tif', target_hot, arrived.astype(jnp.float32), precision=HIGHEST)
        return (local_sum + incoming).astype(jnp.bfloat16).reshape(NODE_DEV, D)

    def pick_rows(grad_tiles, target_dev):
        return grad_tiles[target_dev]

    def node_column(inputs):
        state_col, upstream_col, tiles_col, arrived_col, block_col, adjacency_col, target_col, group_col = inputs
        aggregate = jax.vmap(aggregate_device)(tiles_col, arrived_col, block_col, adjacency_col, target_col)
        row_total = N_GX * NODE_DEV
        flat_state = state_col.reshape(row_total, D)
        aggregate = aggregate.reshape(row_total, D)
        groups = group_col.reshape(row_total)
        coarse = cluster_mean(flat_state, groups)
        node_lifted = (product(flat_state, lift_state) + product(aggregate, lift_agg) + product(coarse, lift_coarse) + node_bias.astype(jnp.float32)).astype(jnp.bfloat16)
        node_active = jax.nn.silu(node_lifted.astype(jnp.float32)).astype(jnp.bfloat16)
        emitted = product(node_active, node_emit)
        center = emitted - lax.optimization_barrier(jnp.mean(emitted, axis=-1, keepdims=True))
        inverse = lax.rsqrt(lax.optimization_barrier(jnp.mean(center * center, axis=-1, keepdims=True)) + NORM_EPS)
        normed = center * inverse
        gain_wide = norm_gain.astype(jnp.float32)
        updated = (flat_state.astype(jnp.float32) + gain_wide * normed).astype(jnp.bfloat16)
        upstream = upstream_col.reshape(row_total, D).astype(jnp.float32)
        gain_grad = lax.optimization_barrier(jnp.sum(upstream * normed, axis=0))
        scaled = upstream * gain_wide
        emit_grad = inverse * (scaled - lax.optimization_barrier(jnp.mean(scaled, axis=-1, keepdims=True)) - normed * lax.optimization_barrier(jnp.mean(scaled * normed, axis=-1, keepdims=True)))
        emit_weight_grad = product_across(node_active.astype(jnp.float32), emit_grad)
        active_grad = product_back(emit_grad, node_emit.astype(jnp.float32)).astype(jnp.bfloat16)
        lifted_grad = (active_grad.astype(jnp.float32) * silu_slope(node_lifted.astype(jnp.float32))).astype(jnp.bfloat16)
        lift_grad = jnp.concatenate([product_across(flat_state, lifted_grad), product_across(aggregate, lifted_grad), product_across(coarse, lifted_grad)], axis=0)
        bias_grad = lax.optimization_barrier(jnp.sum(lifted_grad.astype(jnp.float32), axis=0))
        aggregate_grad = product_back(lifted_grad, lift_agg).astype(jnp.bfloat16)
        coarse_grad = product_back(lifted_grad, lift_coarse).astype(jnp.bfloat16)
        pooled_grad = cluster_mean(coarse_grad, groups)
        state_part = upstream + product_back(lifted_grad, lift_state) + pooled_grad.astype(jnp.float32)
        grad_tiles = aggregate_grad.reshape(N_GX, TILES_DEV, TILE, D)
        returned = jax.vmap(pick_rows)(grad_tiles, target_col)
        return (updated.reshape(N_GX, NODE_DEV, D), state_part.reshape(N_GX, NODE_DEV, D), grad_tiles, returned, (lift_grad, bias_grad, emit_weight_grad, gain_grad))
    updated_all, state_parts, grad_tiles_all, returned_all, node_sums = lax.map(node_column, (states, upstream_all, tiles_all, arrived_all, blocks, neighbours, targets, groups_all))
    sent_back = travel(returned_all, -1)

    def message_device(block_dev, adjacency_dev, grad_tiles, source_dev, cut_dev, back_dev):
        spread = jnp.einsum('tkij,tif->tkjf', block_dev.astype(jnp.float32), grad_tiles.astype(jnp.float32), precision=HIGHEST)
        source_hot = (adjacency_dev[:, :, None] == tile_ids).astype(jnp.float32)
        local_grad = jnp.einsum('tks,tkjf->sjf', source_hot, spread, precision=HIGHEST)
        cut_spread = jnp.einsum('pcij,pcif->pcjf', cut_dev.astype(jnp.float32), back_dev.astype(jnp.float32), precision=HIGHEST)
        cut_hot = (source_dev[:, :, None] == tile_ids).astype(jnp.float32)
        cut_grad = jnp.einsum('pcs,pcjf->sjf', cut_hot, cut_spread, precision=HIGHEST)
        return (local_grad + cut_grad).astype(jnp.bfloat16).reshape(NODE_DEV, D)

    def edge_column(inputs):
        state_col, part_col, block_col, adjacency_col, grad_col, source_col, cut_col, back_col = inputs
        message_grad = jax.vmap(message_device)(block_col, adjacency_col, grad_col, source_col, cut_col, back_col)
        row_total = N_GX * NODE_DEV
        flat_state = state_col.reshape(row_total, D)
        message_grad = message_grad.reshape(row_total, D)
        lifted, active = edge_front(flat_state, edge_lift, edge_bias)
        emit_weight_grad = product_across(active, message_grad)
        edge_active_grad = product_back(message_grad, edge_emit).astype(jnp.bfloat16)
        edge_lifted_grad = (edge_active_grad.astype(jnp.float32) * silu_slope(lifted.astype(jnp.float32))).astype(jnp.bfloat16)
        lift_grad = product_across(flat_state, edge_lifted_grad)
        bias_grad = lax.optimization_barrier(jnp.sum(edge_lifted_grad.astype(jnp.float32), axis=0))
        state_grad = (part_col.reshape(row_total, D) + product_back(edge_lifted_grad, edge_lift)).astype(jnp.bfloat16)
        return (state_grad.reshape(N_GX, NODE_DEV, D), (lift_grad, bias_grad, emit_weight_grad))
    state_grads, edge_sums = lax.map(edge_column, (states, state_parts, blocks, neighbours, grad_tiles_all, sources, cut_all, sent_back))
    grad_scale = NODES ** (-0.5)
    updated = jnp.swapaxes(updated_all, 0, 1).reshape(NODES, D)
    state_grad = jnp.swapaxes(state_grads, 0, 1).reshape(NODES, D)
    return (updated, state_grad, lax.optimization_barrier(jnp.sum(edge_sums[0], axis=0)) * grad_scale, lax.optimization_barrier(jnp.sum(edge_sums[1], axis=0)) * grad_scale, lax.optimization_barrier(jnp.sum(edge_sums[2], axis=0)) * grad_scale, lax.optimization_barrier(jnp.sum(node_sums[0], axis=0)) * grad_scale, lax.optimization_barrier(jnp.sum(node_sums[1], axis=0)) * grad_scale, lax.optimization_barrier(jnp.sum(node_sums[2], axis=0)) * grad_scale, lax.optimization_barrier(jnp.sum(node_sums[3], axis=0)) * grad_scale)
```

```python
import functools

import jax
import jax.numpy as jnp
from jax import lax
from jax.experimental import pallas as pl
from jax.experimental.pallas import tpu as pltpu
from jax.sharding import Mesh
from jax.sharding import PartitionSpec as P

CLUS_DEV = 24
NORM_EPS = 1e-05
TILE = 128
F32 = jnp.float32
BF16 = jnp.bfloat16
VMEM_LIMIT = 24 * 1024 * 1024


def mm(left, right):
    return jnp.dot(left, right, preferred_element_type=F32)


def mm_tn(left, right):
    return lax.dot_general(left, right, (((0,), (0,)), ((), ())), preferred_element_type=F32)


def mm_nt(left, right):
    return lax.dot_general(left, right, (((1,), (1,)), ((), ())), preferred_element_type=F32)


def tile_rows(index):
    return pl.ds(pl.multiple_of(index * TILE, TILE), TILE)


def rows_of(tile):
    return slice(tile * TILE, (tile + 1) * TILE)


def hot_rows(clus_row, first, count):
    ids = lax.broadcasted_iota(jnp.int32, (count, clus_row.shape[1]), 0) + first
    return jnp.where(ids == clus_row, 1.0, 0.0).astype(BF16)


def hot_columns(clus_row, clusters):
    spread = jnp.broadcast_to(clus_row.astype(F32), (TILE, TILE)).T
    spread = jnp.concatenate([spread] * (-(-clusters // TILE)), axis=1)[:, :clusters]
    ids = lax.broadcasted_iota(jnp.int32, (TILE, clusters), 1).astype(F32)
    return jnp.where(ids == spread, 1.0, 0.0).astype(BF16)


def call(kernel, outs, in_specs=None, scratch=(), aliases=None, out_specs=None, flops=0, moved=0):
    options = {}
    if in_specs is not None:
        options["in_specs"] = in_specs
    if out_specs is not None:
        options["out_specs"] = out_specs
    return pl.pallas_call(
        kernel,
        out_shape=outs,
        scratch_shapes=list(scratch),
        input_output_aliases=aliases or {},
        compiler_params=pltpu.CompilerParams(vmem_limit_bytes=VMEM_LIMIT),
        cost_estimate=pl.CostEstimate(flops=flops, bytes_accessed=moved, transcendentals=0),
        **options,
    )


def vmem(count):
    return [pl.BlockSpec(memory_space=pltpu.VMEM)] * count


def smem(count):
    return [pl.BlockSpec(memory_space=pltpu.SMEM)] * count


def like(shape, kind):
    return jax.ShapeDtypeStruct(shape, kind)


def front_kernel(sizes, source, adjacency, clus, state, edge_lift, edge_bias, edge_emit, blocks,
                 cuts, pool, part0, part1, part2, part3, lifted, active, local, message):
    peers, share = sizes
    tiles = state.shape[0] // TILE
    clus_row = clus[...]
    ones = jnp.ones((16, state.shape[0]), BF16)
    low_half = lax.broadcasted_iota(jnp.int32, (16, TILE), 0) >= 8
    bias = edge_bias[...].astype(F32)
    for tile in range(tiles):
        rows = rows_of(tile)
        value = (mm(state[rows], edge_lift[...]) + bias).astype(BF16)
        lifted[rows] = value
        wide = value.astype(F32)
        hidden = (wide * jax.nn.sigmoid(wide)).astype(BF16)
        active[rows] = hidden
        message[rows] = mm(hidden, edge_emit[...]).astype(BF16)
    for slot, part in enumerate((part0, part1, part2, part3)):
        for cut in range(cuts.shape[1]):
            part[rows_of(cut)] = mm(
                cuts[slot, cut], message[tile_rows(source[slot, cut])]
            ).astype(BF16)
    for peer in range(peers):
        hot = hot_rows(clus_row, peer * share, TILE)
        pool[peer, 0:share] = mm(hot, state[...])[:share].astype(BF16)
        count = mm_nt(ones, hot)
        high = jnp.floor(count * (1.0 / 16.0))
        pool[peer, share:share + 16, 0:TILE] = jnp.where(
            low_half, count - 16.0 * high, high
        ).astype(BF16)
        pool[peer, share:share + 16, TILE:] = jnp.zeros((16, state.shape[1] - TILE), BF16)
    for tile in range(tiles):
        total = mm(blocks[tile, 0], message[tile_rows(adjacency[tile, 0])])
        for slot in range(1, blocks.shape[1]):
            total += mm(blocks[tile, slot], message[tile_rows(adjacency[tile, slot])])
        local[rows_of(tile)] = total


def sum_kernel(copies, received, out):
    total = jnp.sum(received[...].astype(F32), axis=0).astype(BF16)
    for index in range(copies):
        out[index] = total


def mean_kernel(share, received, means, counts):
    total = jnp.sum(received[...].astype(F32), axis=0)
    high, low = total[share:share + 1, 0:TILE], total[share + 8:share + 9, 0:TILE]
    count = jnp.broadcast_to(high * 16.0 + low, (TILE, TILE)).T[:share]
    count = jnp.concatenate([count] * (means.shape[1] // TILE), axis=1)
    counts[...] = count
    means[...] = (total[:share] / count).astype(BF16)


def node_kernel(target, clus, state, upstream, local, arrived0, arrived1, arrived2, arrived3,
                means, node_lift, node_bias, node_emit, norm_gain,
                updated, aggregate, coarse, active, emit_grad, lifted_grad, aggregate_grad,
                coarse_grad, back0, back1, back2, back3, vectors, summed):
    features = state.shape[1]
    clusters = means.shape[0]
    summed[...] = local[...]
    for slot, arrived in enumerate((arrived0, arrived1, arrived2, arrived3)):
        for cut in range(arrived.shape[0] // TILE):
            summed[tile_rows(target[slot, cut])] += arrived[rows_of(cut)].astype(F32)
    lift_state = node_lift[0:features]
    lift_agg = node_lift[features:2 * features]
    lift_coarse = node_lift[2 * features:]
    bias = node_bias[...].astype(F32)
    gain = norm_gain[...].astype(F32)
    gain_grad = jnp.zeros((1, features), F32)
    bias_grad = jnp.zeros((1, features), F32)
    for tile in range(state.shape[0] // TILE):
        rows = rows_of(tile)
        here = state[rows]
        agg = summed[rows].astype(BF16)
        aggregate[rows] = agg
        hot = hot_columns(clus[0:1, rows], clusters)
        pooled = mm(hot, means[...]).astype(BF16)
        coarse[rows] = pooled
        lifted = (
            mm(here, lift_state) + mm(agg, lift_agg) + mm(pooled, lift_coarse) + bias
        ).astype(BF16).astype(F32)
        gate = jax.nn.sigmoid(lifted)
        hidden = (lifted * gate).astype(BF16)
        active[rows] = hidden
        emitted = mm(hidden, node_emit[...])
        center = emitted - jnp.mean(emitted, axis=-1, keepdims=True)
        inverse = lax.rsqrt(jnp.mean(center * center, axis=-1, keepdims=True) + NORM_EPS)
        normed = center * inverse
        updated[rows] = (here.astype(F32) + gain * normed).astype(BF16)
        above = upstream[rows].astype(F32)
        gain_grad += jnp.sum(above * normed, axis=0, keepdims=True)
        scaled = above * gain
        grad = (
            inverse
            * (
                scaled
                - jnp.mean(scaled, axis=-1, keepdims=True)
                - normed * jnp.mean(scaled * normed, axis=-1, keepdims=True)
            )
        ).astype(BF16)
        emit_grad[rows] = grad
        active_grad = mm_nt(grad, node_emit[...]).astype(BF16).astype(F32)
        slope = gate * (1.0 + lifted * (1.0 - gate))
        down = (active_grad * slope).astype(BF16)
        lifted_grad[rows] = down
        bias_grad += jnp.sum(down.astype(F32), axis=0, keepdims=True)
        aggregate_grad[rows] = mm_nt(down, lift_agg).astype(BF16)
        coarse_grad[rows] = mm_nt(down, lift_coarse).astype(BF16)
    for slot, back in enumerate((back0, back1, back2, back3)):
        for cut in range(back.shape[0] // TILE):
            back[rows_of(cut)] = aggregate_grad[tile_rows(target[slot, cut])]
    vectors[...] = jnp.zeros(vectors.shape, F32)
    vectors[0:1] = bias_grad
    vectors[1:2] = gain_grad


def put_chunks(packed, first, size, start, value):
    done = 0
    while done < value.shape[0]:
        peer, offset = divmod(start + done, size)
        count = min(size - offset, value.shape[0] - done)
        packed[peer, first + offset:first + offset + count] = value[done:done + count].astype(BF16)
        done += count


def weight_kernel(sizes, adjacency, clus, state, upstream, aggregate, coarse, active, emit_grad,
                  lifted_grad, aggregate_grad, coarse_grad, blocks, node_lift,
                  packed, local, partial):
    peers, share, node_rows, _ = sizes
    features = state.shape[1]
    clus_row = clus[...]
    for peer in range(peers):
        packed[peer, 0:share] = mm(
            hot_rows(clus_row, peer * share, share), coarse_grad[...]
        ).astype(BF16)
    down = lifted_grad[...]
    for index, block in enumerate((state, aggregate, coarse)):
        put_chunks(packed, share, node_rows, index * features, mm_tn(block[...], down))
    put_chunks(packed, share, node_rows, 3 * features, mm_tn(active[...], emit_grad[...]))
    local[...] = jnp.zeros(local.shape, F32)
    for tile in range(state.shape[0] // TILE):
        rows = rows_of(tile)
        for slot in range(blocks.shape[1]):
            local[tile_rows(adjacency[tile, slot])] += mm_tn(
                blocks[tile, slot], aggregate_grad[rows]
            )
        partial[rows] = upstream[rows].astype(F32) + mm_nt(
            lifted_grad[rows], node_lift[0:features]
        )


def edge_kernel(sizes, source, state, lifted, active, local, back0, back1, back2, back3, cuts,
                edge_lift, edge_emit, partial, vectors, packed_in,
                packed, partial_out, total, message_grad, lifted_grad, edge_part, sem):
    peers, share, node_rows, edge_rows = sizes
    features = state.shape[1]
    total[...] = local[...]
    for slot, back in enumerate((back0, back1, back2, back3)):
        for cut in range(cuts.shape[1]):
            total[tile_rows(source[slot, cut])] += mm_tn(cuts[slot, cut], back[rows_of(cut)])
    bias_grad = jnp.zeros((1, features), F32)
    for tile in range(state.shape[0] // TILE):
        rows = rows_of(tile)
        grad = total[rows].astype(BF16)
        message_grad[rows] = grad
        active_grad = mm_nt(grad, edge_emit[...]).astype(BF16).astype(F32)
        wide = lifted[rows].astype(F32)
        gate = jax.nn.sigmoid(wide)
        down = (active_grad * (gate * (1.0 + wide * (1.0 - gate)))).astype(BF16)
        lifted_grad[rows] = down
        bias_grad += jnp.sum(down.astype(F32), axis=0, keepdims=True)
        partial_out[rows] = partial[rows] + mm_nt(down, edge_lift[...])
    put_chunks(edge_part, 0, edge_rows, 0, mm_tn(state[...], lifted_grad[...]))
    put_chunks(edge_part, 0, edge_rows, features, mm_tn(active[...], message_grad[...]))
    edge_part[:, edge_rows:] = jnp.zeros((peers, 16, features), BF16)
    last = lax.broadcasted_iota(jnp.int32, (16, features), 0)
    edge_part[0, edge_rows:] = jnp.where(
        last == 0, vectors[0:1], jnp.where(last == 1, vectors[1:2], jnp.where(last == 2, bias_grad, 0.0))
    ).astype(BF16)
    place = packed.at[:, pl.ds(share + node_rows, edge_rows + 16), :]
    copy = pltpu.make_async_copy(edge_part, place, sem)
    copy.start()
    copy.wait()


def split_kernel(share, received, pool, grads):
    total = jnp.sum(received[...].astype(F32), axis=0)
    pool[...] = total[:share].astype(BF16)
    used = total.shape[0] - share
    chunk = grads.shape[1]
    for index in range(grads.shape[0]):
        first = index * chunk
        count = max(0, min(chunk, used - first))
        if count:
            grads[index, 0:count] = total[share + first:share + first + count].astype(BF16)
        if count < chunk:
            grads[index, count:] = jnp.zeros((chunk - count, total.shape[1]), BF16)


def join_kernel(pool, received, out):
    share = pool.shape[0]
    grads = jnp.sum(received[...].astype(F32), axis=0).astype(BF16)
    for index in range(out.shape[0]):
        out[index, 0:share] = pool[...]
        out[index, share:] = grads


def settle_kernel(share, received, counts, means, grads):
    total = jnp.sum(received[...].astype(F32), axis=0)
    means[...] = (total[:share] / counts[...]).astype(BF16)
    whole = total[share:].astype(BF16)
    for index in range(grads.shape[0]):
        grads[index] = whole


def last_kernel(sizes, scale, clus, partial, gathered, state_grad, edge_lift, edge_bias, edge_emit,
                node_lift, node_bias, node_emit, norm_gain, means):
    peers, share, node_rows, edge_rows = sizes
    features = partial.shape[1]
    for peer in range(peers):
        means[peer * share:(peer + 1) * share] = gathered[peer, 0:share]
    for tile in range(partial.shape[0] // TILE):
        rows = rows_of(tile)
        pooled = mm(hot_columns(clus[0:1, rows], peers * share), means[...])
        state_grad[rows] = (partial[rows] + pooled).astype(BF16)

    def take(first, size, outs):
        for index, out in enumerate(outs):
            start, done = index * features, 0
            height = out.shape[0]
            if index and outs[0].shape[0] != features:
                start = outs[0].shape[0]
            while done < height:
                peer, offset = divmod(start + done, size)
                count = min(size - offset, height - done)
                out[done:done + count] = (
                    gathered[peer, first + offset:first + offset + count].astype(F32) * scale
                )
                done += count

    take(share, node_rows, (node_lift, node_emit))
    take(share + node_rows, edge_rows, (edge_lift, edge_emit))
    tail = gathered[0, share + node_rows + edge_rows:].astype(F32) * scale
    node_bias[...] = tail[0:1]
    norm_gain[...] = tail[1:2]
    edge_bias[...] = tail[2:3]


def shards(
    node_state,
    node_grad,
    edge_blocks,
    adjacency,
    cut_source,
    cut_target,
    cut_blocks,
    clusters,
    edge_lift,
    edge_bias,
    edge_emit,
    node_lift,
    node_bias,
    node_emit,
    norm_gain,
):
    far, peers, columns = (lax.axis_size(name) for name in ("far", "near", "gy"))
    rows, features = node_state.shape
    along = far * peers
    share = CLUS_DEV * far
    node_rows = 4 * features // peers
    edge_rows = 2 * features // peers
    sizes = (peers, share, node_rows, edge_rows)
    packed_rows = share + node_rows + edge_rows + 16
    chunk = -(-(packed_rows - share) // (16 * columns)) * 16
    source, target = cut_source[0, 0], cut_target[0, 0]
    cuts = cut_blocks[0, 0]
    cut_rows = cuts.shape[1] * TILE
    clus = clusters.reshape(1, rows)
    bias_row, node_bias_row, gain_row = (v.reshape(1, features) for v in (edge_bias, node_bias, norm_gain))
    wide = like((rows, features), F32)
    narrow = like((rows, features), BF16)
    cut_part = like((cut_rows, features), BF16)
    layer = 2 * rows * features * features

    def shift(value, axis, steps, count):
        pairs = [(i, i + steps) for i in range(max(0, -steps), min(count, count - steps))]
        return lax.ppermute(value, axis, pairs)

    def travel(parts, direction):
        gx = ("far", "near")
        return [
            shift(parts[0], gx, direction, along),
            shift(parts[1], gx, -direction, along),
            shift(parts[2], "gy", direction, columns),
            shift(parts[3], "gy", -direction, columns),
        ]

    front = call(
        functools.partial(front_kernel, (peers, share)),
        [like((peers, share + 16, features), BF16)] + [cut_part] * 4 + [narrow, narrow, wide],
        smem(2) + vmem(7),
        [pltpu.VMEM((rows, features), BF16)],
        flops=8 * layer,
        moved=4 << 20,
    )
    pool, part0, part1, part2, part3, lifted, active, local = front(
        source, adjacency, clus, node_state, edge_lift, bias_row, edge_emit, edge_blocks, cuts
    )
    arrived = travel([part0, part1, part2, part3], 1)

    received = lax.all_to_all(pool, "near", 0, 0, tiled=True)
    summed = call(
        functools.partial(sum_kernel, far), like((far, share + 16, features), BF16), moved=1 << 20
    )(received)
    received = lax.all_to_all(summed, "far", 0, 0, tiled=True)
    means, counts = call(
        functools.partial(mean_kernel, share),
        [like((share, features), BF16), like((share, features), F32)],
        moved=1 << 20,
    )(received)
    all_means = lax.all_gather(means, "near", axis=0, tiled=True)

    node = call(
        node_kernel,
        [narrow] * 8 + [cut_part] * 4 + [like((8, features), F32)],
        smem(1) + vmem(13),
        [pltpu.VMEM((rows, features), F32)],
        flops=10 * layer,
        moved=4 << 20,
    )
    (updated, aggregate, coarse, node_active, emit_grad, lifted_grad, aggregate_grad, coarse_grad,
     back0, back1, back2, back3, vectors) = node(
        target, clus, node_state, node_grad, local, *arrived, all_means, node_lift, node_bias_row,
        node_emit, gain_row,
    )
    returned = travel([back0, back1, back2, back3], -1)

    weights = call(
        functools.partial(weight_kernel, sizes),
        [like((peers, packed_rows, features), BF16), wide, wide],
        smem(1) + vmem(12),
        flops=8 * layer,
        moved=5 << 20,
    )
    packed, message_local, partial = weights(
        adjacency, clus, node_state, node_grad, aggregate, coarse, node_active, emit_grad,
        lifted_grad, aggregate_grad, coarse_grad, edge_blocks, node_lift,
    )
    anywhere = pl.BlockSpec(memory_space=pl.ANY)
    edge = call(
        functools.partial(edge_kernel, sizes),
        [like((peers, packed_rows, features), BF16), wide],
        smem(1) + vmem(13) + [anywhere],
        [
            pltpu.VMEM((rows, features), F32),
            pltpu.VMEM((rows, features), BF16),
            pltpu.VMEM((rows, features), BF16),
            pltpu.VMEM((peers, edge_rows + 16, features), BF16),
            pltpu.SemaphoreType.DMA,
        ],
        {14: 0},
        [anywhere] + vmem(1),
        flops=8 * layer,
        moved=5 << 20,
    )
    packed, partial = edge(
        source, node_state, lifted, active, message_local, *returned, cuts, edge_lift, edge_emit,
        partial, vectors, packed,
    )

    received = lax.all_to_all(packed, "near", 0, 0, tiled=True)
    pool, grads = call(
        functools.partial(split_kernel, share),
        [like((share, features), BF16), like((columns, chunk, features), BF16)],
        moved=1 << 20,
    )(received)
    received = lax.all_to_all(grads, "gy", 0, 0, tiled=True)
    joined = call(
        join_kernel, like((far, share + chunk, features), BF16), moved=1 << 20
    )(pool, received)
    received = lax.all_to_all(joined, "far", 0, 0, tiled=True)
    means, grads = call(
        functools.partial(settle_kernel, share),
        [like((share, features), BF16), like((columns, chunk, features), BF16)],
        moved=1 << 20,
    )(received, counts)
    grads = lax.all_to_all(grads, "gy", 0, 0, tiled=True).reshape(columns * chunk, features)
    gathered = lax.all_gather(
        jnp.concatenate([means, grads[:packed_rows - share]], axis=0), "near", axis=0, tiled=False
    )
    scale = float(rows * along * columns) ** (-0.5)
    square, line = like((features, features), F32), like((1, features), F32)
    (state_grad, edge_lift_grad, edge_bias_grad, edge_emit_grad, node_lift_grad, node_bias_grad,
     node_emit_grad, gain_grad) = call(
        functools.partial(last_kernel, sizes, scale),
        [narrow, square, line, square, like((3 * features, features), F32), line, square, line],
        vmem(3),
        [pltpu.VMEM((peers * share, features), BF16)],
        flops=3 * layer,
        moved=4 << 20,
    )(clus, partial, gathered)
    return (
        updated,
        state_grad,
        edge_lift_grad,
        edge_bias_grad.reshape(features),
        edge_emit_grad,
        node_lift_grad,
        node_bias_grad.reshape(features),
        node_emit_grad,
        gain_grad.reshape(features),
    )


def solution(mesh):
    gx, gy = mesh.shape["gx"], mesh.shape["gy"]
    near = 8 if gx % 8 == 0 and gx > 8 else 4
    grid = Mesh(mesh.devices.reshape(gx // near, near, gy), ("far", "near", "gy"))
    both, across = ("far", "near", "gy"), ("far", "near")
    placed = (
        P(both, None),
        P(both, None),
        P(both, None, None, None),
        P(both, None),
        P(across, "gy", None, None),
        P(across, "gy", None, None),
        P(across, "gy", None, None, None, None),
        P(both),
        P(),
        P(),
        P(),
        P(),
        P(),
        P(),
        P(),
    )
    return jax.shard_map(
        shards,
        mesh=grid,
        in_specs=placed,
        out_specs=(P(both, None), P(both, None), P(), P(), P(), P(), P(), P(), P()),
        check_vma=False,
    )
```

```python
import functools

import jax
import jax.numpy as jnp
from jax import lax
from jax.experimental import pallas as pl
from jax.experimental.pallas import tpu as pltpu
from jax.sharding import Mesh
from jax.sharding import PartitionSpec as P

CLUS_DEV = 24
NORM_EPS = 1e-05
TILE = 128
F32 = jnp.float32
BF16 = jnp.bfloat16
VMEM_LIMIT = 24 * 1024 * 1024
FIRST_LIMIT = 60 * 1024 * 1024


def mm(left, right):
    return jnp.dot(left, right, preferred_element_type=F32)


def mm_tn(left, right):
    return lax.dot_general(left, right, (((0,), (0,)), ((), ())), preferred_element_type=F32)


def mm_nt(left, right):
    return lax.dot_general(left, right, (((1,), (1,)), ((), ())), preferred_element_type=F32)


def tile_rows(index):
    return pl.ds(pl.multiple_of(index * TILE, TILE), TILE)


def rows_of(tile):
    return slice(tile * TILE, (tile + 1) * TILE)


def hot_rows(clus_row, first, count):
    ids = lax.broadcasted_iota(jnp.int32, (count, clus_row.shape[1]), 0) + first
    return jnp.where(ids == clus_row, 1.0, 0.0).astype(BF16)


def hot_columns(clus_row, clusters):
    spread = jnp.broadcast_to(clus_row.astype(F32), (TILE, TILE)).T
    spread = jnp.concatenate([spread] * (-(-clusters // TILE)), axis=1)[:, :clusters]
    ids = lax.broadcasted_iota(jnp.int32, (TILE, clusters), 1).astype(F32)
    return jnp.where(ids == spread, 1.0, 0.0).astype(BF16)


def slots(side):
    near, gy = lax.axis_index("core"), lax.rem(lax.axis_index("gy"), 2)
    out = (1 - near, 3 - gy, 2 + gy, near)
    return out if side == "out" else (near, 2 + gy, 3 - gy, 1 - near)


def call(kernel, outs, in_specs=None, scratch=(), limit=VMEM_LIMIT, out_specs=None, flops=0, moved=0):
    options = {}
    if in_specs is not None:
        options["in_specs"] = in_specs
    if out_specs is not None:
        options["out_specs"] = out_specs
    return pl.pallas_call(
        kernel,
        out_shape=outs,
        scratch_shapes=list(scratch),
        compiler_params=pltpu.CompilerParams(vmem_limit_bytes=limit),
        cost_estimate=pl.CostEstimate(flops=flops, bytes_accessed=moved, transcendentals=0),
        **options,
    )


def vmem(count):
    return [pl.BlockSpec(memory_space=pltpu.VMEM)] * count


def smem(count):
    return [pl.BlockSpec(memory_space=pltpu.SMEM)] * count


def like(shape, kind):
    return jax.ShapeDtypeStruct(shape, kind)


def front_kernel(share, *refs):
    far, refs = refs[:11], refs[11:]
    (pool, part0, part1, part2, part3, lifted, active, local, params), refs = refs[:9], refs[9:]
    near, (message, sems) = refs[:11], refs[11:]
    copies = [
        pltpu.make_async_copy(*pair, sems.at[index])
        for index, pair in enumerate(zip(far, near))
    ]
    for copy in copies:
        copy.start()
    (clus, state, edge_bias, node_bias, norm_gain, edge_lift, edge_emit, source, adjacency, cuts,
     blocks) = near
    rows, features = state.shape
    tiles = rows // TILE
    for copy in copies[:2]:
        copy.wait()
    clus_row = clus[...]
    ones = jnp.ones((16, rows), BF16)
    line = lax.broadcasted_iota(jnp.int32, (16, TILE), 0)
    for peer in range(pool.shape[0]):
        hot = hot_rows(clus_row, peer * share, TILE)
        pool[peer, 0:share] = mm(hot, state[...])[:share].astype(BF16)
        count = mm_nt(ones, hot)
        eights = jnp.floor(count * 0.125)
        high = jnp.floor(eights * 0.125)
        digits = jnp.where(
            line < 4, count - 8.0 * eights, jnp.where(line < 8, eights - 8.0 * high, high)
        )
        pool[peer, share:share + 16, 0:TILE] = digits.astype(BF16)
        pool[peer, share:share + 16, TILE:] = jnp.zeros((16, features - TILE), BF16)
    for copy in copies[2:]:
        copy.wait()
    params[...] = jnp.zeros(params.shape, F32)
    for index, vector in enumerate((node_bias, norm_gain)):
        params[index:index + 1] = vector[...].astype(F32).reshape(1, -1)
    bias = edge_bias[...].astype(F32).reshape(1, -1)
    for tile in range(tiles):
        rows = rows_of(tile)
        value = (mm(state[rows], edge_lift[...]) + bias).astype(BF16)
        lifted[rows] = value
        wide = value.astype(F32)
        hidden = (wide * jax.nn.sigmoid(wide)).astype(BF16)
        active[rows] = hidden
        message[rows] = mm(hidden, edge_emit[...]).astype(BF16)
    for slot, part in zip(slots("out"), (part0, part1, part2, part3)):
        for cut in range(cuts.shape[1]):
            part[rows_of(cut)] = mm(
                cuts[slot, cut], message[tile_rows(source[cut, slot])]
            ).astype(BF16)
    for tile in range(tiles):
        total = mm(blocks[tile, 0], message[tile_rows(adjacency[tile, 0])])
        for slot in range(1, blocks.shape[1]):
            total += mm(blocks[tile, slot], message[tile_rows(adjacency[tile, slot])])
        local[rows_of(tile)] = total


def aggregate_kernel(target, local, arrived0, arrived1, arrived2, arrived3, aggregate, summed):
    summed[...] = local[...]
    for slot, arrived in zip(slots("in"), (arrived0, arrived1, arrived2, arrived3)):
        for cut in range(arrived.shape[0] // TILE):
            summed[tile_rows(target[cut, slot])] += arrived[rows_of(cut)].astype(F32)
    aggregate[...] = summed[...].astype(BF16)


def sum_kernel(received, out):
    total = jnp.sum(received[...].astype(F32), axis=0).astype(BF16)
    for peer in range(out.shape[0]):
        out[peer] = total


def mean_kernel(share, received, means, counts):
    total = jnp.sum(received[...].astype(F32), axis=0)
    low, middle, high = (total[share + row:share + row + 1, 0:TILE] for row in (0, 4, 8))
    count = jnp.broadcast_to(high * 64.0 + middle * 8.0 + low, (TILE, TILE)).T[:share]
    count = jnp.concatenate([count] * (means.shape[2] // TILE), axis=1)
    counts[...] = count
    mean = (total[:share] / count).astype(BF16)
    for peer in range(means.shape[0]):
        means[peer] = mean


def node_kernel(target, clus, state, upstream, aggregate, mine, other, node_lift, node_emit, params,
                updated, coarse, active, emit_grad, lifted_grad, aggregate_grad,
                coarse_grad, back0, back1, back2, back3, vectors, means):
    features = state.shape[1]
    clusters, share = means.shape[0], mine.shape[1]
    core = lax.axis_index("core")
    for peer in range(clusters // share):
        means[peer * share:(peer + 1) * share] = jnp.where(
            core == peer % 2, mine[peer // 2], other[peer // 2]
        )
    lift_state = node_lift[0:features]
    lift_agg = node_lift[features:2 * features]
    lift_coarse = node_lift[2 * features:]
    bias = params[0:1]
    gain = params[1:2]
    gain_grad = jnp.zeros((1, features), F32)
    bias_grad = jnp.zeros((1, features), F32)
    for tile in range(state.shape[0] // TILE):
        rows = rows_of(tile)
        here = state[rows]
        agg = aggregate[rows]
        hot = hot_columns(clus[0:1, rows], clusters)
        pooled = mm(hot, means[...]).astype(BF16)
        coarse[rows] = pooled
        lifted = (
            mm(here, lift_state) + mm(agg, lift_agg) + mm(pooled, lift_coarse) + bias
        ).astype(BF16).astype(F32)
        gate = jax.nn.sigmoid(lifted)
        hidden = (lifted * gate).astype(BF16)
        active[rows] = hidden
        emitted = mm(hidden, node_emit[...])
        center = emitted - jnp.mean(emitted, axis=-1, keepdims=True)
        inverse = lax.rsqrt(jnp.mean(center * center, axis=-1, keepdims=True) + NORM_EPS)
        normed = center * inverse
        updated[rows] = (here.astype(F32) + gain * normed).astype(BF16)
        above = upstream[rows].astype(F32)
        gain_grad += jnp.sum(above * normed, axis=0, keepdims=True)
        scaled = above * gain
        grad = (
            inverse
            * (
                scaled
                - jnp.mean(scaled, axis=-1, keepdims=True)
                - normed * jnp.mean(scaled * normed, axis=-1, keepdims=True)
            )
        ).astype(BF16)
        emit_grad[rows] = grad
        active_grad = mm_nt(grad, node_emit[...]).astype(BF16).astype(F32)
        slope = gate * (1.0 + lifted * (1.0 - gate))
        down = (active_grad * slope).astype(BF16)
        lifted_grad[rows] = down
        bias_grad += jnp.sum(down.astype(F32), axis=0, keepdims=True)
        aggregate_grad[rows] = mm_nt(down, lift_agg).astype(BF16)
        coarse_grad[rows] = mm_nt(down, lift_coarse).astype(BF16)
    for slot, back in zip(slots("in"), (back0, back1, back2, back3)):
        for cut in range(back.shape[0] // TILE):
            back[rows_of(cut)] = aggregate_grad[tile_rows(target[cut, slot])]
    vectors[...] = jnp.zeros(vectors.shape, F32)
    vectors[0:1] = bias_grad
    vectors[1:2] = gain_grad


def put_chunks(packed, first, size, start, value):
    done = 0
    while done < value.shape[0]:
        peer, offset = divmod(start + done, size)
        count = min(size - offset, value.shape[0] - done)
        packed[peer, first + offset:first + offset + count] = value[done:done + count].astype(BF16)
        done += count


def part_ways(stack, keep, send):
    core = lax.axis_index("core")
    for index in range(keep.shape[0]):
        keep[index] = stack[2 * index + core]
        send[index] = stack[2 * index + 1 - core]


def weight_kernel(sizes, adjacency, clus, state, upstream, aggregate, coarse, active, emit_grad,
                  lifted_grad, aggregate_grad, coarse_grad, blocks, node_lift,
                  keep, send, local, partial, stack):
    peers, share, node_rows, _ = sizes
    features = state.shape[1]
    clus_row = clus[...]
    for peer in range(peers):
        stack[peer, 0:share] = mm(
            hot_rows(clus_row, peer * share, share), coarse_grad[...]
        ).astype(BF16)
    down = lifted_grad[...]
    for index, block in enumerate((state, aggregate, coarse)):
        put_chunks(stack, share, node_rows, index * features, mm_tn(block[...], down))
    put_chunks(stack, share, node_rows, 3 * features, mm_tn(active[...], emit_grad[...]))
    part_ways(stack, keep, send)
    local[...] = jnp.zeros(local.shape, F32)
    for tile in range(state.shape[0] // TILE):
        rows = rows_of(tile)
        for slot in range(blocks.shape[1]):
            local[tile_rows(adjacency[tile, slot])] += mm_tn(
                blocks[tile, slot], aggregate_grad[rows]
            )
        partial[rows] = upstream[rows].astype(F32) + mm_nt(
            lifted_grad[rows], node_lift[0:features]
        )


def edge_kernel(sizes, source, state, lifted, active, local, back0, back1, back2, back3, cuts,
                edge_lift, edge_emit, partial, vectors,
                keep, send, partial_out, total, message_grad, lifted_grad, edge_part):
    peers, _, _, edge_rows = sizes
    features = state.shape[1]
    total[...] = local[...]
    for slot, back in zip(slots("out"), (back0, back1, back2, back3)):
        for cut in range(cuts.shape[1]):
            total[tile_rows(source[cut, slot])] += mm_tn(cuts[slot, cut], back[rows_of(cut)])
    bias_grad = jnp.zeros((1, features), F32)
    for tile in range(state.shape[0] // TILE):
        rows = rows_of(tile)
        grad = total[rows].astype(BF16)
        message_grad[rows] = grad
        active_grad = mm_nt(grad, edge_emit[...]).astype(BF16).astype(F32)
        wide = lifted[rows].astype(F32)
        gate = jax.nn.sigmoid(wide)
        down = (active_grad * (gate * (1.0 + wide * (1.0 - gate)))).astype(BF16)
        lifted_grad[rows] = down
        bias_grad += jnp.sum(down.astype(F32), axis=0, keepdims=True)
        partial_out[rows] = partial[rows] + mm_nt(down, edge_lift[...])
    put_chunks(edge_part, 0, edge_rows, 0, mm_tn(state[...], lifted_grad[...]))
    put_chunks(edge_part, 0, edge_rows, features, mm_tn(active[...], message_grad[...]))
    edge_part[:, edge_rows:] = jnp.zeros((peers, 16, features), BF16)
    last = lax.broadcasted_iota(jnp.int32, (16, features), 0)
    edge_part[0, edge_rows:] = jnp.where(
        last == 0, vectors[0:1], jnp.where(last == 1, vectors[1:2], jnp.where(last == 2, bias_grad, 0.0))
    ).astype(BF16)
    part_ways(edge_part, keep, send)


def merge_kernel(keep_node, keep_edge, got_node, got_edge, out):
    rows = keep_node.shape[1]
    out[:, 0:rows] = (keep_node[...].astype(F32) + got_node[...].astype(F32)).astype(BF16)
    out[:, rows:] = (keep_edge[...].astype(F32) + got_edge[...].astype(F32)).astype(BF16)


def split_kernel(share, received, pool, grads):
    total = jnp.sum(received[...].astype(F32), axis=0).astype(BF16)
    pool[...] = total[:share]
    chunk = grads.shape[1]
    row = 0
    while row < total.shape[0] - share:
        index, offset = divmod(row, chunk)
        grads[index, offset:offset + 16] = total[share + row:share + row + 16]
        row += 16
    while row < grads.shape[0] * chunk:
        index, offset = divmod(row, chunk)
        grads[index, offset:offset + 16] = jnp.zeros((16, grads.shape[2]), BF16)
        row += 16


def join_kernel(pool, received, out):
    share = pool.shape[0]
    grads = jnp.sum(received[...].astype(F32), axis=0).astype(BF16)
    for peer in range(out.shape[0]):
        out[peer, 0:share] = pool[...]
        out[peer, share:] = grads


def settle_kernel(share, received, counts, means, grads):
    total = jnp.sum(received[...].astype(F32), axis=0)
    means[...] = (total[:share] / counts[...]).astype(BF16)
    whole = total[share:].astype(BF16)
    for index in range(grads.shape[0]):
        grads[index] = whole


def spread_kernel(means, grads, out):
    share, used = means.shape[0], out.shape[1] - means.shape[0]
    chunk = grads.shape[1]
    for peer in range(out.shape[0]):
        out[peer, 0:share] = means[...]
        for first in range(0, used, chunk):
            count = min(chunk, used - first)
            out[peer, share + first:share + first + count] = grads[first // chunk, 0:count]


def last_kernel(sizes, scale, clus, partial, mine, other, state_grad, edge_lift, edge_bias,
                edge_emit, node_lift, node_bias, node_emit, norm_gain, means):
    peers, share, node_rows, edge_rows = sizes
    features = partial.shape[1]
    core = lax.axis_index("core")

    def gathered(peer, first, count):
        rows = slice(first, first + count)
        return jnp.where(core == peer % 2, mine[peer // 2, rows], other[peer // 2, rows])

    for peer in range(peers):
        means[peer * share:(peer + 1) * share] = gathered(peer, 0, share)
    for tile in range(partial.shape[0] // TILE):
        rows = rows_of(tile)
        pooled = mm(hot_columns(clus[0:1, rows], peers * share), means[...])
        state_grad[rows] = (partial[rows] + pooled).astype(BF16)

    def take(first, size, outs):
        start = 0
        for out in outs:
            done = 0
            while done < out.shape[0]:
                peer, offset = divmod(start + done, size)
                count = min(size - offset, out.shape[0] - done)
                out[done:done + count] = gathered(peer, first + offset, count).astype(F32) * scale
                done += count
            start += done

    take(share, node_rows, (node_lift, node_emit))
    take(share + node_rows, edge_rows, (edge_lift, edge_emit))
    tail = gathered(0, share + node_rows + edge_rows, 16).astype(F32) * scale
    node_bias[...] = tail[0:1]
    norm_gain[...] = tail[1:2]
    edge_bias[...] = tail[2:3]


def shards(
    node_state,
    node_grad,
    edge_blocks,
    adjacency,
    cut_source,
    cut_target,
    cut_blocks,
    clusters,
    edge_lift,
    edge_bias,
    edge_emit,
    node_lift,
    node_bias,
    node_emit,
    norm_gain,
):
    near = ("y", "core")
    far, across, columns = (lax.axis_size(name) for name in ("far", "y", "gy"))
    peers = 2 * across
    rows, features = node_state.shape
    along = far * peers
    share = CLUS_DEV * far
    node_rows = 4 * features // peers
    edge_rows = 2 * features // peers
    sizes = (peers, share, node_rows, edge_rows)
    packed_rows = share + node_rows + edge_rows + 16
    chunk = -(-(packed_rows - share) // (16 * columns)) * 16
    source, target = cut_source[0, 0].T, cut_target[0, 0].T
    cuts = cut_blocks[0, 0]
    cut_rows = cuts.shape[1] * TILE
    clus = clusters.reshape(1, rows)
    wide = like((rows, features), F32)
    narrow = like((rows, features), BF16)
    cut_part = like((cut_rows, features), BF16)
    layer = 2 * rows * features * features

    gx = ("far", *near)
    both_cores = [(0, 1), (1, 0)]

    def swap(parts):
        moved = []
        for part, axis, count, first in zip(
            parts, (gx, "gy", "gy", gx), (along, columns, columns, along), (1, 1, 0, 0)
        ):
            pairs = [(i, i + 1) for i in range(first, count - 1, 2)]
            moved.append(lax.ppermute(part, axis, pairs + [(j, i) for i, j in pairs]))
        return moved

    operands = (clus, node_state, edge_bias, node_bias, norm_gain, edge_lift, edge_emit, source,
                adjacency, cuts, edge_blocks)
    tables = (source, adjacency)
    pool, part0, part1, part2, part3, lifted, active, local, params = call(
        functools.partial(front_kernel, share),
        [like((peers, share + 16, features), BF16)] + [cut_part] * 4
        + [narrow, narrow, wide, like((8, features), F32)],
        [pl.BlockSpec(memory_space=pl.ANY)] * len(operands),
        [
            (pltpu.SMEM if any(v is table for table in tables) else pltpu.VMEM)(v.shape, v.dtype)
            for v in operands
        ]
        + [pltpu.VMEM((rows, features), BF16), pltpu.SemaphoreType.DMA((len(operands),))],
        FIRST_LIMIT,
        out_specs=vmem(9),
        flops=8 * layer,
        moved=4 << 20,
    )(*operands)
    received = lax.all_to_all(pool, near, 0, 0, tiled=True)
    summed = call(
        sum_kernel,
        like((far, share + 16, features), BF16),
        vmem(1),
        out_specs=pl.BlockSpec(memory_space=pltpu.VMEM),
        moved=1 << 20,
    )(received)
    arrived = swap((part0, part1, part2, part3))
    received = lax.all_to_all(summed, "far", 0, 0, tiled=True)
    received, *arrived = lax.optimization_barrier((received, *arrived))
    means, counts = call(
        functools.partial(mean_kernel, share),
        [like((across, share, features), BF16), like((share, features), F32)],
        vmem(1),
        out_specs=vmem(2),
        moved=1 << 20,
    )(received)
    my_means = lax.all_to_all(means, "y", 0, 0, tiled=True)
    other_means = lax.ppermute(my_means, "core", both_cores)
    local, my_means, *arrived = lax.optimization_barrier((local, my_means, *arrived))
    aggregate = call(
        aggregate_kernel,
        narrow,
        smem(1) + vmem(5),
        [pltpu.VMEM((rows, features), F32)],
        moved=2 << 20,
    )(target, local, *arrived)

    (updated, coarse, node_active, emit_grad, lifted_grad, aggregate_grad, coarse_grad,
     back0, back1, back2, back3, vectors) = call(
        node_kernel,
        [narrow] * 7 + [cut_part] * 4 + [like((8, features), F32)],
        smem(1) + vmem(9),
        [pltpu.VMEM((peers * share, features), BF16)],
        flops=10 * layer,
        moved=4 << 20,
    )(target, clus, node_state, node_grad, aggregate, my_means, other_means, node_lift, node_emit,
      params)

    keep_node, send_node, message_local, partial = call(
        functools.partial(weight_kernel, sizes),
        [like((across, share + node_rows, features), BF16)] * 2 + [wide, wide],
        smem(1) + vmem(12),
        [pltpu.VMEM((peers, share + node_rows, features), BF16)],
        flops=8 * layer,
        moved=5 << 20,
    )(adjacency, clus, node_state, node_grad, aggregate, coarse, node_active, emit_grad,
      lifted_grad, aggregate_grad, coarse_grad, edge_blocks, node_lift)
    returned = swap((back0, back1, back2, back3))
    send_node, *returned = lax.optimization_barrier((send_node, *returned))
    got_node = lax.ppermute(send_node, "core", both_cores)
    keep_edge, send_edge, partial = call(
        functools.partial(edge_kernel, sizes),
        [like((across, edge_rows + 16, features), BF16)] * 2 + [wide],
        smem(1) + vmem(13),
        [
            pltpu.VMEM((rows, features), F32),
            pltpu.VMEM((rows, features), BF16),
            pltpu.VMEM((rows, features), BF16),
            pltpu.VMEM((peers, edge_rows + 16, features), BF16),
        ],
        flops=8 * layer,
        moved=5 << 20,
    )(source, node_state, lifted, active, message_local, *returned, cuts, edge_lift, edge_emit,
      partial, vectors)
    got_edge = lax.ppermute(send_edge, "core", both_cores)
    merged = call(
        merge_kernel, like((across, packed_rows, features), BF16), vmem(4), moved=2 << 20
    )(keep_node, keep_edge, got_node, got_edge)
    received = lax.all_to_all(merged, "y", 0, 0, tiled=True)
    pool, grads = call(
        functools.partial(split_kernel, share),
        [like((share, features), BF16), like((columns, chunk, features), BF16)],
        vmem(1),
        moved=1 << 20,
    )(received)
    received = lax.all_to_all(grads, "gy", 0, 0, tiled=True)
    joined = call(
        join_kernel, like((far, share + chunk, features), BF16), vmem(2), moved=1 << 20
    )(pool, received)
    received = lax.all_to_all(joined, "far", 0, 0, tiled=True)
    means, grads = call(
        functools.partial(settle_kernel, share),
        [like((share, features), BF16), like((columns, chunk, features), BF16)],
        vmem(2),
        moved=1 << 20,
    )(received, counts)
    grads = lax.all_to_all(grads, "gy", 0, 0, tiled=True)
    spread = call(
        spread_kernel, like((across, packed_rows, features), BF16), vmem(2), moved=2 << 20
    )(means, grads)
    mine = lax.all_to_all(spread, "y", 0, 0, tiled=True)
    other = lax.ppermute(mine, "core", both_cores)
    scale = float(rows * along * columns) ** (-0.5)
    square, line = like((features, features), F32), like((1, features), F32)
    (state_grad, edge_lift_grad, edge_bias_grad, edge_emit_grad, node_lift_grad, node_bias_grad,
     node_emit_grad, gain_grad) = call(
        functools.partial(last_kernel, sizes, scale),
        [narrow, square, line, square, like((3 * features, features), F32), line, square, line],
        vmem(4),
        [pltpu.VMEM((peers * share, features), BF16)],
        flops=3 * layer,
        moved=4 << 20,
    )(clus, partial, mine, other)
    return (
        updated,
        state_grad,
        edge_lift_grad,
        edge_bias_grad.reshape(features),
        edge_emit_grad,
        node_lift_grad,
        node_bias_grad.reshape(features),
        node_emit_grad,
        gain_grad.reshape(features),
    )


def solution(mesh):
    gx, gy = mesh.shape["gx"], mesh.shape["gy"]
    near = 8 if gx % 8 == 0 and gx > 8 else 4
    grid = Mesh(
        mesh.devices.reshape(gx // near, near // 2, 2, gy), ("far", "y", "core", "gy")
    )
    across = ("far", "y", "core")
    both = (*across, "gy")
    placed = (
        P(both, None),
        P(both, None),
        P(both, None, None, None),
        P(both, None),
        P(across, "gy", None, None),
        P(across, "gy", None, None),
        P(across, "gy", None, None, None, None),
        P(both),
        P(),
        P(),
        P(),
        P(),
        P(),
        P(),
        P(),
    )
    return jax.shard_map(
        shards,
        mesh=grid,
        in_specs=placed,
        out_specs=(P(both, None), P(both, None), P(), P(), P(), P(), P(), P(), P()),
        check_vma=False,
    )
```

```python
import functools

import jax
import jax.numpy as jnp
from jax import lax
from jax.experimental import pallas as pl
from jax.experimental.pallas import tpu as pltpu
from jax.sharding import Mesh
from jax.sharding import PartitionSpec as P

CLUS_DEV = 24
NORM_EPS = 1e-05
TILE = 128
F32 = jnp.float32
BF16 = jnp.bfloat16
VMEM_LIMIT = 24 * 1024 * 1024
FIRST_LIMIT = 60 * 1024 * 1024


def mm(left, right):
    return jnp.dot(left, right, preferred_element_type=F32)


def mm_tn(left, right):
    return lax.dot_general(left, right, (((0,), (0,)), ((), ())), preferred_element_type=F32)


def mm_nt(left, right):
    return lax.dot_general(left, right, (((1,), (1,)), ((), ())), preferred_element_type=F32)


def tile_rows(index):
    return pl.ds(pl.multiple_of(index * TILE, TILE), TILE)


def rows_of(tile):
    return slice(tile * TILE, (tile + 1) * TILE)


def hot_rows(clus_row, first, count):
    ids = lax.broadcasted_iota(jnp.int32, (count, clus_row.shape[1]), 0) + first
    return jnp.where(ids == clus_row, 1.0, 0.0).astype(BF16)


def hot_columns(clus_row, clusters):
    spread = jnp.broadcast_to(clus_row.astype(F32), (TILE, TILE)).T
    spread = jnp.concatenate([spread] * (-(-clusters // TILE)), axis=1)[:, :clusters]
    ids = lax.broadcasted_iota(jnp.int32, (TILE, clusters), 1).astype(F32)
    return jnp.where(ids == spread, 1.0, 0.0).astype(BF16)


def slots(side):
    near, gy = lax.axis_index("core"), lax.rem(lax.axis_index("gy"), 2)
    out = (1 - near, 3 - gy, 2 + gy, near)
    return out if side == "out" else (near, 2 + gy, 3 - gy, 1 - near)


def call(kernel, outs, in_specs=None, scratch=(), limit=VMEM_LIMIT, out_specs=None, flops=0, moved=0):
    options = {}
    if in_specs is not None:
        options["in_specs"] = in_specs
    if out_specs is not None:
        options["out_specs"] = out_specs
    return pl.pallas_call(
        kernel,
        out_shape=outs,
        scratch_shapes=list(scratch),
        compiler_params=pltpu.CompilerParams(vmem_limit_bytes=limit),
        cost_estimate=pl.CostEstimate(flops=flops, bytes_accessed=moved, transcendentals=0),
        **options,
    )


def vmem(count):
    return [pl.BlockSpec(memory_space=pltpu.VMEM)] * count


def smem(count):
    return [pl.BlockSpec(memory_space=pltpu.SMEM)] * count


def like(shape, kind):
    return jax.ShapeDtypeStruct(shape, kind)


def front_kernel(share, *refs):
    far, refs = refs[:11], refs[11:]
    (pool, part0, part1, part2, part3, lifted, active, local, params), refs = refs[:9], refs[9:]
    near, (message, hot, sems) = refs[:11], refs[11:]
    copies = [
        pltpu.make_async_copy(*pair, sems.at[index])
        for index, pair in enumerate(zip(far, near))
    ]
    for copy in copies:
        copy.start()
    (clus, state, edge_bias, node_bias, norm_gain, edge_lift, edge_emit, source, adjacency, cuts,
     blocks) = near
    rows, features = state.shape
    tiles = rows // TILE
    for copy in copies[:2]:
        copy.wait()
    clus_row = clus[...]
    line = lax.broadcasted_iota(jnp.int32, (16, TILE), 0)
    for peer in range(pool.shape[0]):
        hot[rows_of(peer)] = hot_rows(clus_row, peer * share, TILE)
    sums = mm(hot[...], state[...])
    counts = mm_nt(jnp.ones((16, rows), BF16), hot[...])
    for peer in range(pool.shape[0]):
        pool[peer, 0:share] = sums[peer * TILE:peer * TILE + share].astype(BF16)
        count = counts[:, rows_of(peer)]
        eights = jnp.floor(count * 0.125)
        high = jnp.floor(eights * 0.125)
        digits = jnp.where(
            line < 4, count - 8.0 * eights, jnp.where(line < 8, eights - 8.0 * high, high)
        )
        pool[peer, share:share + 16, 0:TILE] = digits.astype(BF16)
        pool[peer, share:share + 16, TILE:] = jnp.zeros((16, features - TILE), BF16)
    for copy in copies[2:]:
        copy.wait()
    params[...] = jnp.zeros(params.shape, F32)
    for index, vector in enumerate((node_bias, norm_gain)):
        params[index:index + 1] = vector[...].astype(F32).reshape(1, -1)
    bias = edge_bias[...].astype(F32).reshape(1, -1)
    value = (mm(state[...], edge_lift[...]) + bias).astype(BF16)
    lifted[...] = value
    wide = value.astype(F32)
    hidden = (wide * jax.nn.sigmoid(wide)).astype(BF16)
    active[...] = hidden
    message[...] = mm(hidden, edge_emit[...]).astype(BF16)
    for slot, part in zip(slots("out"), (part0, part1, part2, part3)):
        for cut in range(cuts.shape[1]):
            part[rows_of(cut)] = mm(
                cuts[slot, cut], message[tile_rows(source[cut, slot])]
            ).astype(BF16)
    for tile in range(tiles):
        total = mm(blocks[tile, 0], message[tile_rows(adjacency[tile, 0])])
        for slot in range(1, blocks.shape[1]):
            total += mm(blocks[tile, slot], message[tile_rows(adjacency[tile, slot])])
        local[rows_of(tile)] = total


def aggregate_kernel(target, local, arrived0, arrived1, arrived2, arrived3, aggregate, summed):
    summed[...] = local[...]
    for slot, arrived in zip(slots("in"), (arrived0, arrived1, arrived2, arrived3)):
        for cut in range(arrived.shape[0] // TILE):
            summed[tile_rows(target[cut, slot])] += arrived[rows_of(cut)].astype(F32)
    aggregate[...] = summed[...].astype(BF16)


def sum_kernel(received, out):
    out[...] = jnp.sum(received[...].astype(F32), axis=0).astype(BF16)


def add_kernel(mine, other, out):
    out[...] = (mine[...].astype(F32) + other[...].astype(F32)).astype(BF16)


def mean_kernel(share, mine, other, means, counts):
    total = mine[...].astype(F32) + other[...].astype(F32)
    low, middle, high = (total[share + row:share + row + 1, 0:TILE] for row in (0, 4, 8))
    count = jnp.broadcast_to(high * 64.0 + middle * 8.0 + low, (TILE, TILE)).T[:share]
    count = jnp.concatenate([count] * (means.shape[2] // TILE), axis=1)
    counts[...] = count
    mean = (total[:share] / count).astype(BF16)
    for peer in range(means.shape[0]):
        means[peer] = mean


def node_kernel(target, clus, state, upstream, aggregate, mine, other, node_lift, node_emit, params,
                updated, coarse, active, emit_grad, lifted_grad, aggregate_grad,
                coarse_grad, back0, back1, back2, vectors, means, slopes, hot):
    features = state.shape[1]
    clusters, share = means.shape[0], mine.shape[1]
    core = lax.axis_index("core")
    for peer in range(clusters // share):
        means[peer * share:(peer + 1) * share] = jnp.where(
            core == peer % 2, mine[peer // 2], other[peer // 2]
        )
    lift_state = node_lift[0:features]
    lift_agg = node_lift[features:2 * features]
    lift_coarse = node_lift[2 * features:]
    bias = params[0:1]
    gain = params[1:2]
    gain_grad = jnp.zeros((1, features), F32)
    bias_grad = jnp.zeros((1, features), F32)
    here = state[...]
    for tile in range(state.shape[0] // TILE):
        hot[rows_of(tile)] = hot_columns(clus[0:1, rows_of(tile)], clusters)
    coarse[...] = mm(hot[...], means[...]).astype(BF16)
    lifted = (
        mm(here, lift_state) + mm(aggregate[...], lift_agg) + mm(coarse[...], lift_coarse)
        + bias
    ).astype(BF16).astype(F32)
    gate = jax.nn.sigmoid(lifted)
    hidden = (lifted * gate).astype(BF16)
    active[...] = hidden
    slopes[...] = gate * (1.0 + lifted * (1.0 - gate))
    emitted = mm(hidden, node_emit[...])
    center = emitted - jnp.mean(emitted, axis=-1, keepdims=True)
    inverse = lax.rsqrt(jnp.mean(center * center, axis=-1, keepdims=True) + NORM_EPS)
    normed = center * inverse
    updated[...] = (here.astype(F32) + gain * normed).astype(BF16)
    above = upstream[...].astype(F32)
    gain_grad += jnp.sum(above * normed, axis=0, keepdims=True)
    scaled = above * gain
    grad = (
        inverse
        * (
            scaled
            - jnp.mean(scaled, axis=-1, keepdims=True)
            - normed * jnp.mean(scaled * normed, axis=-1, keepdims=True)
        )
    ).astype(BF16)
    emit_grad[...] = grad
    active_grad = mm_nt(grad, node_emit[...]).astype(BF16).astype(F32)
    down = (active_grad * slopes[...]).astype(BF16)
    lifted_grad[...] = down
    bias_grad += jnp.sum(down.astype(F32), axis=0, keepdims=True)
    aggregate_grad[...] = mm_nt(down, lift_agg).astype(BF16)
    coarse_grad[...] = mm_nt(down, lift_coarse).astype(BF16)
    for slot, back in zip(slots("in"), (back0, back1, back2)):
        for cut in range(back.shape[0] // TILE):
            back[rows_of(cut)] = aggregate_grad[tile_rows(target[cut, slot])]
    vectors[...] = jnp.zeros(vectors.shape, F32)
    vectors[0:1] = bias_grad
    vectors[1:2] = gain_grad


def put_chunks(packed, first, size, start, value):
    done = 0
    while done < value.shape[0]:
        peer, offset = divmod(start + done, size)
        count = min(size - offset, value.shape[0] - done)
        packed[peer, first + offset:first + offset + count] = value[done:done + count].astype(BF16)
        done += count


def part_ways(stack, keep, send):
    core = lax.axis_index("core")
    for index in range(keep.shape[0]):
        keep[index] = stack[2 * index + core]
        send[index, 0:stack.shape[1]] = stack[2 * index + 1 - core]


def weight_kernel(sizes, adjacency, target, clus, state, upstream, aggregate, coarse, active,
                  emit_grad, lifted_grad, aggregate_grad, coarse_grad, blocks, node_lift,
                  keep, send, local, partial, stack, hot):
    peers, share, node_rows, _ = sizes
    features = state.shape[1]
    clus_row = clus[...]
    for peer in range(peers):
        hot[peer * share:(peer + 1) * share] = hot_rows(clus_row, peer * share, share)
    put_chunks(stack, 0, share, 0, mm(hot[...], coarse_grad[...]))
    down = lifted_grad[...]
    for index, block in enumerate((state, aggregate, coarse)):
        put_chunks(stack, share, node_rows, index * features, mm_tn(block[...], down))
    put_chunks(stack, share, node_rows, 3 * features, mm_tn(active[...], emit_grad[...]))
    part_ways(stack, keep, send)
    each, last = send.shape[1] - keep.shape[1], slots("in")[3]
    for index in range(send.shape[0]):
        cut, row = divmod(index * each, TILE)
        start = pl.multiple_of(target[cut, last] * TILE + row, each)
        send[index, keep.shape[1]:] = aggregate_grad[pl.ds(start, each)]
    partial[...] = upstream[...].astype(F32) + mm_nt(down, node_lift[0:features])
    local[...] = jnp.zeros(local.shape, F32)
    for tile in range(state.shape[0] // TILE):
        rows = rows_of(tile)
        for slot in range(blocks.shape[1]):
            local[tile_rows(adjacency[tile, slot])] += mm_tn(
                blocks[tile, slot], aggregate_grad[rows]
            )


def edge_kernel(sizes, source, state, lifted, active, local, back0, back1, back2, got_node, cuts,
                edge_lift, edge_emit, partial, vectors,
                keep, send, partial_out, total, message_grad, lifted_grad, edge_part):
    peers, share, node_rows, edge_rows = sizes
    features = state.shape[1]
    total[...] = local[...]
    first = share + node_rows
    back3 = jnp.concatenate([got_node[index, first:] for index in range(got_node.shape[0])], axis=0)
    for slot, back in zip(slots("out"), (back0, back1, back2, back3)):
        for cut in range(cuts.shape[1]):
            total[tile_rows(source[cut, slot])] += mm_tn(cuts[slot, cut], back[rows_of(cut)])
    grad = total[...].astype(BF16)
    message_grad[...] = grad
    active_grad = mm_nt(grad, edge_emit[...]).astype(BF16).astype(F32)
    wide = lifted[...].astype(F32)
    gate = jax.nn.sigmoid(wide)
    down = (active_grad * (gate * (1.0 + wide * (1.0 - gate)))).astype(BF16)
    lifted_grad[...] = down
    bias_grad = jnp.sum(down.astype(F32), axis=0, keepdims=True)
    partial_out[...] = partial[...] + mm_nt(down, edge_lift[...])
    put_chunks(edge_part, 0, edge_rows, 0, mm_tn(state[...], lifted_grad[...]))
    put_chunks(edge_part, 0, edge_rows, features, mm_tn(active[...], message_grad[...]))
    edge_part[:, edge_rows:] = jnp.zeros((peers, 16, features), BF16)
    last = lax.broadcasted_iota(jnp.int32, (16, features), 0)
    edge_part[0, edge_rows:] = jnp.where(
        last == 0, vectors[0:1], jnp.where(last == 1, vectors[1:2], jnp.where(last == 2, bias_grad, 0.0))
    ).astype(BF16)
    part_ways(edge_part, keep, send)


def merge_kernel(keep_node, keep_edge, got_node, got_edge, out):
    rows = keep_node.shape[1]
    out[:, 0:rows] = (
        keep_node[...].astype(F32) + got_node[:, 0:rows].astype(F32)
    ).astype(BF16)
    out[:, rows:] = (keep_edge[...].astype(F32) + got_edge[...].astype(F32)).astype(BF16)


def split_kernel(share, received, pool, grads):
    total = jnp.sum(received[...].astype(F32), axis=0).astype(BF16)
    pool[...] = total[:share]
    chunk = grads.shape[1]
    row = 0
    while row < total.shape[0] - share:
        index, offset = divmod(row, chunk)
        grads[index, offset:offset + 16] = total[share + row:share + row + 16]
        row += 16
    while row < grads.shape[0] * chunk:
        index, offset = divmod(row, chunk)
        grads[index, offset:offset + 16] = jnp.zeros((16, grads.shape[2]), BF16)
        row += 16


def join_kernel(pool, received, out):
    share = pool.shape[0]
    grads = jnp.sum(received[...].astype(F32), axis=0).astype(BF16)
    for peer in range(out.shape[0]):
        out[peer, 0:share] = pool[...]
        out[peer, share:] = grads


def settle_kernel(share, received, counts, means, grads):
    total = jnp.sum(received[...].astype(F32), axis=0)
    means[...] = (total[:share] / counts[...]).astype(BF16)
    whole = total[share:].astype(BF16)
    for index in range(grads.shape[0]):
        grads[index] = whole


def spread_kernel(means, grads, out):
    share, used = means.shape[0], out.shape[1] - means.shape[0]
    chunk = grads.shape[1]
    for peer in range(out.shape[0]):
        out[peer, 0:share] = means[...]
        for first in range(0, used, chunk):
            count = min(chunk, used - first)
            out[peer, share + first:share + first + count] = grads[first // chunk, 0:count]


def last_kernel(sizes, scale, clus, partial, mine, other, state_grad, edge_lift, edge_bias,
                edge_emit, node_lift, node_bias, node_emit, norm_gain, means, hot):
    peers, share, node_rows, edge_rows = sizes
    features = partial.shape[1]
    core = lax.axis_index("core")

    def gathered(peer, first, count):
        rows = slice(first, first + count)
        return jnp.where(core == peer % 2, mine[peer // 2, rows], other[peer // 2, rows])

    for peer in range(peers):
        means[peer * share:(peer + 1) * share] = gathered(peer, 0, share)
    for tile in range(partial.shape[0] // TILE):
        rows = rows_of(tile)
        hot[rows] = hot_columns(clus[0:1, rows], peers * share)
    state_grad[...] = (partial[...] + mm(hot[...], means[...])).astype(BF16)

    def take(first, size, outs):
        start = 0
        for out in outs:
            done = 0
            while done < out.shape[0]:
                peer, offset = divmod(start + done, size)
                count = min(size - offset, out.shape[0] - done)
                out[done:done + count] = gathered(peer, first + offset, count).astype(F32) * scale
                done += count
            start += done

    take(share, node_rows, (node_lift, node_emit))
    take(share + node_rows, edge_rows, (edge_lift, edge_emit))
    tail = gathered(0, share + node_rows + edge_rows, 16).astype(F32) * scale
    node_bias[...] = tail[0:1]
    norm_gain[...] = tail[1:2]
    edge_bias[...] = tail[2:3]


def shards(
    node_state,
    node_grad,
    edge_blocks,
    adjacency,
    cut_source,
    cut_target,
    cut_blocks,
    clusters,
    edge_lift,
    edge_bias,
    edge_emit,
    node_lift,
    node_bias,
    node_emit,
    norm_gain,
):
    near = ("y", "core")
    far, across, columns = (lax.axis_size(name) for name in ("far", "y", "gy"))
    peers = 2 * across
    rows, features = node_state.shape
    along = far * peers
    share = CLUS_DEV * far
    node_rows = 4 * features // peers
    edge_rows = 2 * features // peers
    sizes = (peers, share, node_rows, edge_rows)
    packed_rows = share + node_rows + edge_rows + 16
    chunk = -(-(packed_rows - share) // (16 * columns)) * 16
    source, target = cut_source[0, 0].T, cut_target[0, 0].T
    cuts = cut_blocks[0, 0]
    cut_rows = cuts.shape[1] * TILE
    clus = clusters.reshape(1, rows)
    wide = like((rows, features), F32)
    narrow = like((rows, features), BF16)
    cut_part = like((cut_rows, features), BF16)
    layer = 2 * rows * features * features

    gx = ("far", *near)
    both_cores = [(0, 1), (1, 0)]

    ways = ((gx, along, 1), ("gy", columns, 1), ("gy", columns, 0), (gx, along, 0))

    def swap(parts, ways=ways):
        moved = []
        for part, (axis, count, first) in zip(parts, ways):
            pairs = [(i, i + 1) for i in range(first, count - 1, 2)]
            moved.append(lax.ppermute(part, axis, pairs + [(j, i) for i, j in pairs]))
        return moved

    operands = (clus, node_state, edge_bias, node_bias, norm_gain, edge_lift, edge_emit, source,
                adjacency, cuts, edge_blocks)
    tables = (source, adjacency)
    pool, part0, part1, part2, part3, lifted, active, local, params = call(
        functools.partial(front_kernel, share),
        [like((peers, share + 16, features), BF16)] + [cut_part] * 4
        + [narrow, narrow, wide, like((8, features), F32)],
        [pl.BlockSpec(memory_space=pl.ANY)] * len(operands),
        [
            (pltpu.SMEM if any(v is table for table in tables) else pltpu.VMEM)(v.shape, v.dtype)
            for v in operands
        ]
        + [
            pltpu.VMEM((rows, features), BF16),
            pltpu.VMEM((peers * TILE, rows), BF16),
            pltpu.SemaphoreType.DMA((len(operands),)),
        ],
        FIRST_LIMIT,
        out_specs=vmem(9),
        flops=8 * layer,
        moved=4 << 20,
    )(*operands)
    received = lax.all_to_all(pool, near, 0, 0, tiled=True)
    summed = call(
        sum_kernel,
        like((share + 16, features), BF16),
        vmem(1),
        out_specs=pl.BlockSpec(memory_space=pltpu.VMEM),
        moved=1 << 20,
    )(received)
    meetings = [[(i, i ^ 1) for i in range(far)], [(i, far - 1 - i) for i in range(far)]]
    summed, part0, part1 = lax.optimization_barrier((summed, part0, part1))
    other = lax.ppermute(summed, "far", meetings[0])
    arrived = swap((part0, part1), ways[:2])
    if far > 2:
        summed = call(add_kernel, like(summed.shape, BF16), vmem(2), moved=1 << 18)(summed, other)
        summed, part2, part3 = lax.optimization_barrier((summed, part2, part3))
        other = lax.ppermute(summed, "far", meetings[1])
    arrived += swap((part2, part3), ways[2:])
    summed, other, *arrived = lax.optimization_barrier((summed, other, *arrived))
    means, counts = call(
        functools.partial(mean_kernel, share),
        [like((across, share, features), BF16), like((share, features), F32)],
        vmem(2),
        out_specs=vmem(2),
        moved=1 << 20,
    )(summed, other)
    my_means = lax.all_to_all(means, "y", 0, 0, tiled=True)
    other_means = lax.ppermute(my_means, "core", both_cores)
    local, my_means, *arrived = lax.optimization_barrier((local, my_means, *arrived))
    aggregate = call(
        aggregate_kernel,
        narrow,
        smem(1) + vmem(5),
        [pltpu.VMEM((rows, features), F32)],
        moved=2 << 20,
    )(target, local, *arrived)

    (updated, coarse, node_active, emit_grad, lifted_grad, aggregate_grad, coarse_grad,
     back0, back1, back2, vectors) = call(
        node_kernel,
        [narrow] * 7 + [cut_part] * 3 + [like((8, features), F32)],
        smem(1) + vmem(9),
        [
            pltpu.VMEM((peers * share, features), BF16),
            pltpu.VMEM((rows, features), F32),
            pltpu.VMEM((rows, peers * share), BF16),
        ],
        flops=10 * layer,
        moved=4 << 20,
    )(target, clus, node_state, node_grad, aggregate, my_means, other_means, node_lift, node_emit,
      params)

    keep_node, send_node, message_local, partial = call(
        functools.partial(weight_kernel, sizes),
        [
            like((across, share + node_rows, features), BF16),
            like((across, share + node_rows + cut_rows // across, features), BF16),
            wide,
            wide,
        ],
        smem(2) + vmem(12),
        [
            pltpu.VMEM((peers, share + node_rows, features), BF16),
            pltpu.VMEM((peers * share, rows), BF16),
        ],
        flops=8 * layer,
        moved=5 << 20,
    )(adjacency, target, clus, node_state, node_grad, aggregate, coarse, node_active, emit_grad,
      lifted_grad, aggregate_grad, coarse_grad, edge_blocks, node_lift)
    returned = swap((back0, back1, back2))
    got_node = lax.ppermute(send_node, "core", both_cores)
    keep_edge, send_edge, partial = call(
        functools.partial(edge_kernel, sizes),
        [like((across, edge_rows + 16, features), BF16)] * 2 + [wide],
        smem(1) + vmem(13),
        [
            pltpu.VMEM((rows, features), F32),
            pltpu.VMEM((rows, features), BF16),
            pltpu.VMEM((rows, features), BF16),
            pltpu.VMEM((peers, edge_rows + 16, features), BF16),
        ],
        flops=8 * layer,
        moved=5 << 20,
    )(source, node_state, lifted, active, message_local, *returned, got_node, cuts, edge_lift, edge_emit,
      partial, vectors)
    got_edge = lax.ppermute(send_edge, "core", both_cores)
    merged = call(
        merge_kernel, like((across, packed_rows, features), BF16), vmem(4), moved=2 << 20
    )(keep_node, keep_edge, got_node, got_edge)
    received = lax.all_to_all(merged, "y", 0, 0, tiled=True)
    pool, grads = call(
        functools.partial(split_kernel, share),
        [like((share, features), BF16), like((columns, chunk, features), BF16)],
        vmem(1),
        moved=1 << 20,
    )(received)
    received = lax.all_to_all(grads, "gy", 0, 0, tiled=True)
    joined = call(
        join_kernel, like((far, share + chunk, features), BF16), vmem(2), moved=1 << 20
    )(pool, received)
    received = lax.all_to_all(joined, "far", 0, 0, tiled=True)
    means, grads = call(
        functools.partial(settle_kernel, share),
        [like((share, features), BF16), like((columns, chunk, features), BF16)],
        vmem(2),
        moved=1 << 20,
    )(received, counts)
    grads = lax.all_to_all(grads, "gy", 0, 0, tiled=True)
    spread = call(
        spread_kernel, like((across, packed_rows, features), BF16), vmem(2), moved=2 << 20
    )(means, grads)
    mine = lax.all_to_all(spread, "y", 0, 0, tiled=True)
    other = lax.ppermute(mine, "core", both_cores)
    scale = float(rows * along * columns) ** (-0.5)
    square, line = like((features, features), F32), like((1, features), F32)
    (state_grad, edge_lift_grad, edge_bias_grad, edge_emit_grad, node_lift_grad, node_bias_grad,
     node_emit_grad, gain_grad) = call(
        functools.partial(last_kernel, sizes, scale),
        [narrow, square, line, square, like((3 * features, features), F32), line, square, line],
        vmem(4),
        [pltpu.VMEM((peers * share, features), BF16), pltpu.VMEM((rows, peers * share), BF16)],
        flops=3 * layer,
        moved=4 << 20,
    )(clus, partial, mine, other)
    return (
        updated,
        state_grad,
        edge_lift_grad,
        edge_bias_grad.reshape(features),
        edge_emit_grad,
        node_lift_grad,
        node_bias_grad.reshape(features),
        node_emit_grad,
        gain_grad.reshape(features),
    )


def solution(mesh):
    gx, gy = mesh.shape["gx"], mesh.shape["gy"]
    near = 8 if gx % 8 == 0 and gx > 8 else 4
    grid = Mesh(
        mesh.devices.reshape(gx // near, near // 2, 2, gy), ("far", "y", "core", "gy")
    )
    across = ("far", "y", "core")
    both = (*across, "gy")
    placed = (
        P(both, None),
        P(both, None),
        P(both, None, None, None),
        P(both, None),
        P(across, "gy", None, None),
        P(across, "gy", None, None),
        P(across, "gy", None, None, None, None),
        P(both),
        P(),
        P(),
        P(),
        P(),
        P(),
        P(),
        P(),
    )
    return jax.shard_map(
        shards,
        mesh=grid,
        in_specs=placed,
        out_specs=(P(both, None), P(both, None), P(), P(), P(), P(), P(), P(), P()),
        check_vma=False,
    )
```

```python
import functools

import jax
import jax.numpy as jnp
from jax import lax
from jax.experimental import pallas as pl
from jax.experimental.pallas import tpu as pltpu
from jax.sharding import Mesh
from jax.sharding import PartitionSpec as P

CLUS_DEV = 24
NORM_EPS = 1e-05
TILE = 128
F32 = jnp.float32
BF16 = jnp.bfloat16
VMEM_LIMIT = 24 * 1024 * 1024
FIRST_LIMIT = 60 * 1024 * 1024


def mm(left, right):
    return jnp.dot(left, right, preferred_element_type=F32)


def mm_tn(left, right):
    return lax.dot_general(left, right, (((0,), (0,)), ((), ())), preferred_element_type=F32)


def mm_nt(left, right):
    return lax.dot_general(left, right, (((1,), (1,)), ((), ())), preferred_element_type=F32)


def tile_rows(index):
    return pl.ds(pl.multiple_of(index * TILE, TILE), TILE)


def rows_of(tile):
    return slice(tile * TILE, (tile + 1) * TILE)


def hot_rows(clus_row, first, count):
    ids = lax.broadcasted_iota(jnp.int32, (count, clus_row.shape[1]), 0) + first
    return jnp.where(ids == clus_row, 1.0, 0.0).astype(BF16)


def hot_columns(clus_row, clusters):
    spread = jnp.broadcast_to(clus_row.astype(F32), (TILE, TILE)).T
    spread = jnp.concatenate([spread] * (-(-clusters // TILE)), axis=1)[:, :clusters]
    ids = lax.broadcasted_iota(jnp.int32, (TILE, clusters), 1).astype(F32)
    return jnp.where(ids == spread, 1.0, 0.0).astype(BF16)


def slots(side):
    near, gy = lax.axis_index("core"), lax.rem(lax.axis_index("gy"), 2)
    out = (1 - near, 3 - gy, 2 + gy, near)
    return out if side == "out" else (near, 2 + gy, 3 - gy, 1 - near)


def call(kernel, outs, in_specs=None, scratch=(), limit=VMEM_LIMIT, out_specs=None, flops=0, moved=0):
    options = {}
    if in_specs is not None:
        options["in_specs"] = in_specs
    if out_specs is not None:
        options["out_specs"] = out_specs
    return pl.pallas_call(
        kernel,
        out_shape=outs,
        scratch_shapes=list(scratch),
        compiler_params=pltpu.CompilerParams(vmem_limit_bytes=limit),
        cost_estimate=pl.CostEstimate(flops=flops, bytes_accessed=moved, transcendentals=0),
        **options,
    )


def vmem(count):
    return [pl.BlockSpec(memory_space=pltpu.VMEM)] * count


def smem(count):
    return [pl.BlockSpec(memory_space=pltpu.SMEM)] * count


def like(shape, kind):
    return jax.ShapeDtypeStruct(shape, kind)


def front_kernel(share, *refs):
    far, refs = refs[:11], refs[11:]
    (pool, part0, part1, part2, part3, lifted, active, local, params), refs = refs[:9], refs[9:]
    near, (message, hot, sems) = refs[:11], refs[11:]
    copies = [
        pltpu.make_async_copy(*pair, sems.at[index])
        for index, pair in enumerate(zip(far, near))
    ]
    for copy in copies:
        copy.start()
    (clus, state, edge_bias, node_bias, norm_gain, edge_lift, edge_emit, source, adjacency, cuts,
     blocks) = near
    rows, features = state.shape
    tiles = rows // TILE
    for copy in copies[:2]:
        copy.wait()
    clus_row = clus[...]
    line = lax.broadcasted_iota(jnp.int32, (16, TILE), 0)
    for peer in range(pool.shape[0]):
        hot[rows_of(peer)] = hot_rows(clus_row, peer * share, TILE)
    sums = mm(hot[...], state[...])
    counts = mm_nt(jnp.ones((16, rows), BF16), hot[...])
    for peer in range(pool.shape[0]):
        pool[peer, 0:share] = sums[peer * TILE:peer * TILE + share].astype(BF16)
        count = counts[:, rows_of(peer)]
        eights = jnp.floor(count * 0.125)
        high = jnp.floor(eights * 0.125)
        digits = jnp.where(
            line < 4, count - 8.0 * eights, jnp.where(line < 8, eights - 8.0 * high, high)
        )
        pool[peer, share:share + 16, 0:TILE] = digits.astype(BF16)
        pool[peer, share:share + 16, TILE:] = jnp.zeros((16, features - TILE), BF16)
    for copy in copies[2:]:
        copy.wait()
    params[...] = jnp.zeros(params.shape, F32)
    for index, vector in enumerate((node_bias, norm_gain)):
        params[index:index + 1] = vector[...].astype(F32).reshape(1, -1)
    bias = edge_bias[...].astype(F32).reshape(1, -1)
    value = (mm(state[...], edge_lift[...]) + bias).astype(BF16)
    lifted[...] = value
    wide = value.astype(F32)
    hidden = (wide * jax.nn.sigmoid(wide)).astype(BF16)
    active[...] = hidden
    message[...] = mm(hidden, edge_emit[...]).astype(BF16)
    for slot, part in zip(slots("out"), (part0, part1, part2, part3)):
        for cut in range(cuts.shape[1]):
            part[rows_of(cut)] = mm(
                cuts[slot, cut], message[tile_rows(source[cut, slot])]
            ).astype(BF16)
    for tile in range(tiles):
        total = mm(blocks[tile, 0], message[tile_rows(adjacency[tile, 0])])
        for slot in range(1, blocks.shape[1]):
            total += mm(blocks[tile, slot], message[tile_rows(adjacency[tile, slot])])
        local[rows_of(tile)] = total


def aggregate_kernel(target, local, arrived0, arrived1, arrived2, arrived3, aggregate, summed):
    summed[...] = local[...]
    for slot, arrived in zip(slots("in"), (arrived0, arrived1, arrived2, arrived3)):
        for cut in range(arrived.shape[0] // TILE):
            summed[tile_rows(target[cut, slot])] += arrived[rows_of(cut)].astype(F32)
    aggregate[...] = summed[...].astype(BF16)


def sum_kernel(received, out):
    out[...] = jnp.sum(received[...].astype(F32), axis=0).astype(BF16)


def add_kernel(mine, other, out):
    out[...] = (mine[...].astype(F32) + other[...].astype(F32)).astype(BF16)


def mean_kernel(share, mine, other, means, counts):
    total = mine[...].astype(F32) + other[...].astype(F32)
    low, middle, high = (total[share + row:share + row + 1, 0:TILE] for row in (0, 4, 8))
    count = jnp.broadcast_to(high * 64.0 + middle * 8.0 + low, (TILE, TILE)).T[:share]
    count = jnp.concatenate([count] * (means.shape[2] // TILE), axis=1)
    counts[...] = count
    mean = (total[:share] / count).astype(BF16)
    for peer in range(means.shape[0]):
        means[peer] = mean


def node_kernel(target, clus, state, upstream, aggregate, mine, other, node_lift, node_emit, params,
                updated, coarse, active, emit_grad, lifted_grad, aggregate_grad,
                coarse_grad, back0, back1, back2, back3, vectors, means, slopes, hot):
    features = state.shape[1]
    clusters, share = means.shape[0], mine.shape[1]
    core = lax.axis_index("core")
    for peer in range(clusters // share):
        means[peer * share:(peer + 1) * share] = jnp.where(
            core == peer % 2, mine[peer // 2], other[peer // 2]
        )
    lift_state = node_lift[0:features]
    lift_agg = node_lift[features:2 * features]
    lift_coarse = node_lift[2 * features:]
    bias = params[0:1]
    gain = params[1:2]
    gain_grad = jnp.zeros((1, features), F32)
    bias_grad = jnp.zeros((1, features), F32)
    here = state[...]
    for tile in range(state.shape[0] // TILE):
        hot[rows_of(tile)] = hot_columns(clus[0:1, rows_of(tile)], clusters)
    coarse[...] = mm(hot[...], means[...]).astype(BF16)
    lifted = (
        mm(here, lift_state) + mm(aggregate[...], lift_agg) + mm(coarse[...], lift_coarse)
        + bias
    ).astype(BF16).astype(F32)
    gate = jax.nn.sigmoid(lifted)
    hidden = (lifted * gate).astype(BF16)
    active[...] = hidden
    slopes[...] = gate * (1.0 + lifted * (1.0 - gate))
    emitted = mm(hidden, node_emit[...])
    center = emitted - jnp.mean(emitted, axis=-1, keepdims=True)
    inverse = lax.rsqrt(jnp.mean(center * center, axis=-1, keepdims=True) + NORM_EPS)
    normed = center * inverse
    updated[...] = (here.astype(F32) + gain * normed).astype(BF16)
    above = upstream[...].astype(F32)
    gain_grad += jnp.sum(above * normed, axis=0, keepdims=True)
    scaled = above * gain
    grad = (
        inverse
        * (
            scaled
            - jnp.mean(scaled, axis=-1, keepdims=True)
            - normed * jnp.mean(scaled * normed, axis=-1, keepdims=True)
        )
    ).astype(BF16)
    emit_grad[...] = grad
    active_grad = mm_nt(grad, node_emit[...]).astype(BF16).astype(F32)
    down = (active_grad * slopes[...]).astype(BF16)
    lifted_grad[...] = down
    bias_grad += jnp.sum(down.astype(F32), axis=0, keepdims=True)
    aggregate_grad[...] = mm_nt(down, lift_agg).astype(BF16)
    coarse_grad[...] = mm_nt(down, lift_coarse).astype(BF16)
    for slot, back in zip(slots("in"), (back0, back1, back2, back3)):
        for cut in range(back.shape[0] // TILE):
            back[rows_of(cut)] = aggregate_grad[tile_rows(target[cut, slot])]
    vectors[...] = jnp.zeros(vectors.shape, F32)
    vectors[0:1] = bias_grad
    vectors[1:2] = gain_grad


def put_chunks(packed, first, size, start, value):
    done = 0
    while done < value.shape[0]:
        peer, offset = divmod(start + done, size)
        count = min(size - offset, value.shape[0] - done)
        packed[peer, first + offset:first + offset + count] = value[done:done + count].astype(BF16)
        done += count


def part_ways(stack, keep, send):
    core = lax.axis_index("core")
    for index in range(keep.shape[0]):
        keep[index] = stack[2 * index + core]
        send[index] = stack[2 * index + 1 - core]


def weight_kernel(sizes, adjacency, clus, state, upstream, aggregate, coarse, active, emit_grad,
                  lifted_grad, aggregate_grad, coarse_grad, blocks, node_lift,
                  keep, send, local, partial, stack, hot):
    peers, share, node_rows, _ = sizes
    features = state.shape[1]
    clus_row = clus[...]
    for peer in range(peers):
        hot[peer * share:(peer + 1) * share] = hot_rows(clus_row, peer * share, share)
    put_chunks(stack, 0, share, 0, mm(hot[...], coarse_grad[...]))
    down = lifted_grad[...]
    for index, block in enumerate((state, aggregate, coarse)):
        put_chunks(stack, share, node_rows, index * features, mm_tn(block[...], down))
    put_chunks(stack, share, node_rows, 3 * features, mm_tn(active[...], emit_grad[...]))
    part_ways(stack, keep, send)
    partial[...] = upstream[...].astype(F32) + mm_nt(down, node_lift[0:features])
    local[...] = jnp.zeros(local.shape, F32)
    for tile in range(state.shape[0] // TILE):
        rows = rows_of(tile)
        for slot in range(blocks.shape[1]):
            local[tile_rows(adjacency[tile, slot])] += mm_tn(
                blocks[tile, slot], aggregate_grad[rows]
            )


def edge_kernel(sizes, source, state, lifted, active, local, back0, back1, back2, back3, cuts,
                edge_lift, edge_emit, partial, vectors,
                keep, send, partial_out, total, message_grad, lifted_grad, edge_part):
    peers, _, _, edge_rows = sizes
    features = state.shape[1]
    total[...] = local[...]
    for slot, back in zip(slots("out"), (back0, back1, back2, back3)):
        for cut in range(cuts.shape[1]):
            total[tile_rows(source[cut, slot])] += mm_tn(cuts[slot, cut], back[rows_of(cut)])
    grad = total[...].astype(BF16)
    message_grad[...] = grad
    active_grad = mm_nt(grad, edge_emit[...]).astype(BF16).astype(F32)
    wide = lifted[...].astype(F32)
    gate = jax.nn.sigmoid(wide)
    down = (active_grad * (gate * (1.0 + wide * (1.0 - gate)))).astype(BF16)
    lifted_grad[...] = down
    bias_grad = jnp.sum(down.astype(F32), axis=0, keepdims=True)
    partial_out[...] = partial[...] + mm_nt(down, edge_lift[...])
    put_chunks(edge_part, 0, edge_rows, 0, mm_tn(state[...], lifted_grad[...]))
    put_chunks(edge_part, 0, edge_rows, features, mm_tn(active[...], message_grad[...]))
    edge_part[:, edge_rows:] = jnp.zeros((peers, 16, features), BF16)
    last = lax.broadcasted_iota(jnp.int32, (16, features), 0)
    edge_part[0, edge_rows:] = jnp.where(
        last == 0, vectors[0:1], jnp.where(last == 1, vectors[1:2], jnp.where(last == 2, bias_grad, 0.0))
    ).astype(BF16)
    part_ways(edge_part, keep, send)


def merge_kernel(keep_node, keep_edge, got_node, got_edge, out):
    rows = keep_node.shape[1]
    out[:, 0:rows] = (keep_node[...].astype(F32) + got_node[...].astype(F32)).astype(BF16)
    out[:, rows:] = (keep_edge[...].astype(F32) + got_edge[...].astype(F32)).astype(BF16)


def split_kernel(share, received, pool, grads):
    total = jnp.sum(received[...].astype(F32), axis=0).astype(BF16)
    pool[...] = total[:share]
    chunk = grads.shape[1]
    row = 0
    while row < total.shape[0] - share:
        index, offset = divmod(row, chunk)
        grads[index, offset:offset + 16] = total[share + row:share + row + 16]
        row += 16
    while row < grads.shape[0] * chunk:
        index, offset = divmod(row, chunk)
        grads[index, offset:offset + 16] = jnp.zeros((16, grads.shape[2]), BF16)
        row += 16


def join_kernel(pool, received, out):
    share = pool.shape[0]
    grads = jnp.sum(received[...].astype(F32), axis=0).astype(BF16)
    for peer in range(out.shape[0]):
        out[peer, 0:share] = pool[...]
        out[peer, share:] = grads


def settle_kernel(share, received, counts, means, grads):
    total = jnp.sum(received[...].astype(F32), axis=0)
    means[...] = (total[:share] / counts[...]).astype(BF16)
    whole = total[share:].astype(BF16)
    for index in range(grads.shape[0]):
        grads[index] = whole


def spread_kernel(means, grads, out):
    share, used = means.shape[0], out.shape[1] - means.shape[0]
    chunk = grads.shape[1]
    for peer in range(out.shape[0]):
        out[peer, 0:share] = means[...]
        for first in range(0, used, chunk):
            count = min(chunk, used - first)
            out[peer, share + first:share + first + count] = grads[first // chunk, 0:count]


def last_kernel(sizes, scale, clus, partial, mine, other, state_grad, edge_lift, edge_bias,
                edge_emit, node_lift, node_bias, node_emit, norm_gain, means, hot):
    peers, share, node_rows, edge_rows = sizes
    features = partial.shape[1]
    core = lax.axis_index("core")

    def gathered(peer, first, count):
        rows = slice(first, first + count)
        return jnp.where(core == peer % 2, mine[peer // 2, rows], other[peer // 2, rows])

    for peer in range(peers):
        means[peer * share:(peer + 1) * share] = gathered(peer, 0, share)
    for tile in range(partial.shape[0] // TILE):
        rows = rows_of(tile)
        hot[rows] = hot_columns(clus[0:1, rows], peers * share)
    state_grad[...] = (partial[...] + mm(hot[...], means[...])).astype(BF16)

    def take(first, size, outs):
        start = 0
        for out in outs:
            done = 0
            while done < out.shape[0]:
                peer, offset = divmod(start + done, size)
                count = min(size - offset, out.shape[0] - done)
                out[done:done + count] = gathered(peer, first + offset, count).astype(F32) * scale
                done += count
            start += done

    take(share, node_rows, (node_lift, node_emit))
    take(share + node_rows, edge_rows, (edge_lift, edge_emit))
    tail = gathered(0, share + node_rows + edge_rows, 16).astype(F32) * scale
    node_bias[...] = tail[0:1]
    norm_gain[...] = tail[1:2]
    edge_bias[...] = tail[2:3]


def shards(
    node_state,
    node_grad,
    edge_blocks,
    adjacency,
    cut_source,
    cut_target,
    cut_blocks,
    clusters,
    edge_lift,
    edge_bias,
    edge_emit,
    node_lift,
    node_bias,
    node_emit,
    norm_gain,
):
    near = ("y", "core")
    far, across, columns = (lax.axis_size(name) for name in ("far", "y", "gy"))
    peers = 2 * across
    rows, features = node_state.shape
    along = far * peers
    share = CLUS_DEV * far
    node_rows = 4 * features // peers
    edge_rows = 2 * features // peers
    sizes = (peers, share, node_rows, edge_rows)
    packed_rows = share + node_rows + edge_rows + 16
    chunk = -(-(packed_rows - share) // (16 * columns)) * 16
    source, target = cut_source[0, 0].T, cut_target[0, 0].T
    cuts = cut_blocks[0, 0]
    cut_rows = cuts.shape[1] * TILE
    clus = clusters.reshape(1, rows)
    wide = like((rows, features), F32)
    narrow = like((rows, features), BF16)
    cut_part = like((cut_rows, features), BF16)
    layer = 2 * rows * features * features

    gx = ("far", *near)
    both_cores = [(0, 1), (1, 0)]

    ways = ((gx, along, 1), ("gy", columns, 1), ("gy", columns, 0), (gx, along, 0))

    def swap(parts, ways=ways):
        moved = []
        for part, (axis, count, first) in zip(parts, ways):
            pairs = [(i, i + 1) for i in range(first, count - 1, 2)]
            moved.append(lax.ppermute(part, axis, pairs + [(j, i) for i, j in pairs]))
        return moved

    operands = (clus, node_state, edge_bias, node_bias, norm_gain, edge_lift, edge_emit, source,
                adjacency, cuts, edge_blocks)
    tables = (source, adjacency)
    pool, part0, part1, part2, part3, lifted, active, local, params = call(
        functools.partial(front_kernel, share),
        [like((peers, share + 16, features), BF16)] + [cut_part] * 4
        + [narrow, narrow, wide, like((8, features), F32)],
        [pl.BlockSpec(memory_space=pl.ANY)] * len(operands),
        [
            (pltpu.SMEM if any(v is table for table in tables) else pltpu.VMEM)(v.shape, v.dtype)
            for v in operands
        ]
        + [
            pltpu.VMEM((rows, features), BF16),
            pltpu.VMEM((peers * TILE, rows), BF16),
            pltpu.SemaphoreType.DMA((len(operands),)),
        ],
        FIRST_LIMIT,
        out_specs=vmem(9),
        flops=8 * layer,
        moved=4 << 20,
    )(*operands)
    received = lax.all_to_all(pool, near, 0, 0, tiled=True)
    summed = call(
        sum_kernel,
        like((share + 16, features), BF16),
        vmem(1),
        out_specs=pl.BlockSpec(memory_space=pltpu.VMEM),
        moved=1 << 20,
    )(received)
    meetings = [[(i, i ^ 1) for i in range(far)], [(i, far - 1 - i) for i in range(far)]]
    summed, part0, part1 = lax.optimization_barrier((summed, part0, part1))
    other = lax.ppermute(summed, "far", meetings[0])
    arrived = swap((part0, part1), ways[:2])
    if far > 2:
        summed = call(add_kernel, like(summed.shape, BF16), vmem(2), moved=1 << 18)(summed, other)
        summed, part2, part3 = lax.optimization_barrier((summed, part2, part3))
        other = lax.ppermute(summed, "far", meetings[1])
    arrived += swap((part2, part3), ways[2:])
    summed, other, *arrived = lax.optimization_barrier((summed, other, *arrived))
    means, counts = call(
        functools.partial(mean_kernel, share),
        [like((across, share, features), BF16), like((share, features), F32)],
        vmem(2),
        out_specs=vmem(2),
        moved=1 << 20,
    )(summed, other)
    my_means = lax.all_to_all(means, "y", 0, 0, tiled=True)
    other_means = lax.ppermute(my_means, "core", both_cores)
    local, my_means, *arrived = lax.optimization_barrier((local, my_means, *arrived))
    aggregate = call(
        aggregate_kernel,
        narrow,
        smem(1) + vmem(5),
        [pltpu.VMEM((rows, features), F32)],
        moved=2 << 20,
    )(target, local, *arrived)

    (updated, coarse, node_active, emit_grad, lifted_grad, aggregate_grad, coarse_grad,
     back0, back1, back2, back3, vectors) = call(
        node_kernel,
        [narrow] * 7 + [cut_part] * 4 + [like((8, features), F32)],
        smem(1) + vmem(9),
        [
            pltpu.VMEM((peers * share, features), BF16),
            pltpu.VMEM((rows, features), F32),
            pltpu.VMEM((rows, peers * share), BF16),
        ],
        flops=10 * layer,
        moved=4 << 20,
    )(target, clus, node_state, node_grad, aggregate, my_means, other_means, node_lift, node_emit,
      params)

    keep_node, send_node, message_local, partial = call(
        functools.partial(weight_kernel, sizes),
        [like((across, share + node_rows, features), BF16)] * 2 + [wide, wide],
        smem(1) + vmem(12),
        [
            pltpu.VMEM((peers, share + node_rows, features), BF16),
            pltpu.VMEM((peers * share, rows), BF16),
        ],
        flops=8 * layer,
        moved=5 << 20,
    )(adjacency, clus, node_state, node_grad, aggregate, coarse, node_active, emit_grad,
      lifted_grad, aggregate_grad, coarse_grad, edge_blocks, node_lift)
    returned = swap((back0, back1, back2, back3))
    send_node, *returned = lax.optimization_barrier((send_node, *returned))
    got_node = lax.ppermute(send_node, "core", both_cores)
    keep_edge, send_edge, partial = call(
        functools.partial(edge_kernel, sizes),
        [like((across, edge_rows + 16, features), BF16)] * 2 + [wide],
        smem(1) + vmem(13),
        [
            pltpu.VMEM((rows, features), F32),
            pltpu.VMEM((rows, features), BF16),
            pltpu.VMEM((rows, features), BF16),
            pltpu.VMEM((peers, edge_rows + 16, features), BF16),
        ],
        flops=8 * layer,
        moved=5 << 20,
    )(source, node_state, lifted, active, message_local, *returned, cuts, edge_lift, edge_emit,
      partial, vectors)
    got_edge = lax.ppermute(send_edge, "core", both_cores)
    merged = call(
        merge_kernel, like((across, packed_rows, features), BF16), vmem(4), moved=2 << 20
    )(keep_node, keep_edge, got_node, got_edge)
    received = lax.all_to_all(merged, "y", 0, 0, tiled=True)
    pool, grads = call(
        functools.partial(split_kernel, share),
        [like((share, features), BF16), like((columns, chunk, features), BF16)],
        vmem(1),
        moved=1 << 20,
    )(received)
    received = lax.all_to_all(grads, "gy", 0, 0, tiled=True)
    joined = call(
        join_kernel, like((far, share + chunk, features), BF16), vmem(2), moved=1 << 20
    )(pool, received)
    received = lax.all_to_all(joined, "far", 0, 0, tiled=True)
    means, grads = call(
        functools.partial(settle_kernel, share),
        [like((share, features), BF16), like((columns, chunk, features), BF16)],
        vmem(2),
        moved=1 << 20,
    )(received, counts)
    grads = lax.all_to_all(grads, "gy", 0, 0, tiled=True)
    spread = call(
        spread_kernel, like((across, packed_rows, features), BF16), vmem(2), moved=2 << 20
    )(means, grads)
    mine = lax.all_to_all(spread, "y", 0, 0, tiled=True)
    other = lax.ppermute(mine, "core", both_cores)
    scale = float(rows * along * columns) ** (-0.5)
    square, line = like((features, features), F32), like((1, features), F32)
    (state_grad, edge_lift_grad, edge_bias_grad, edge_emit_grad, node_lift_grad, node_bias_grad,
     node_emit_grad, gain_grad) = call(
        functools.partial(last_kernel, sizes, scale),
        [narrow, square, line, square, like((3 * features, features), F32), line, square, line],
        vmem(4),
        [pltpu.VMEM((peers * share, features), BF16), pltpu.VMEM((rows, peers * share), BF16)],
        flops=3 * layer,
        moved=4 << 20,
    )(clus, partial, mine, other)
    return (
        updated,
        state_grad,
        edge_lift_grad,
        edge_bias_grad.reshape(features),
        edge_emit_grad,
        node_lift_grad,
        node_bias_grad.reshape(features),
        node_emit_grad,
        gain_grad.reshape(features),
    )


def solution(mesh):
    gx, gy = mesh.shape["gx"], mesh.shape["gy"]
    near = 8 if gx % 8 == 0 and gx > 8 else 4
    grid = Mesh(
        mesh.devices.reshape(gx // near, near // 2, 2, gy), ("far", "y", "core", "gy")
    )
    across = ("far", "y", "core")
    both = (*across, "gy")
    placed = (
        P(both, None),
        P(both, None),
        P(both, None, None, None),
        P(both, None),
        P(across, "gy", None, None),
        P(across, "gy", None, None),
        P(across, "gy", None, None, None, None),
        P(both),
        P(),
        P(),
        P(),
        P(),
        P(),
        P(),
        P(),
    )
    return jax.shard_map(
        shards,
        mesh=grid,
        in_specs=placed,
        out_specs=(P(both, None), P(both, None), P(), P(), P(), P(), P(), P(), P()),
        check_vma=False,
    )
```

```python
import functools

import jax
import jax.numpy as jnp
from jax import lax
from jax.experimental import pallas as pl
from jax.experimental.pallas import tpu as pltpu
from jax.sharding import Mesh
from jax.sharding import PartitionSpec as P

CLUS_DEV = 24
NORM_EPS = 1e-05
TILE = 128
F32 = jnp.float32
BF16 = jnp.bfloat16
VMEM_LIMIT = 24 * 1024 * 1024
FIRST_LIMIT = 60 * 1024 * 1024


def mm(left, right):
    return jnp.dot(left, right, preferred_element_type=F32)


def mm_tn(left, right):
    return lax.dot_general(left, right, (((0,), (0,)), ((), ())), preferred_element_type=F32)


def mm_nt(left, right):
    return lax.dot_general(left, right, (((1,), (1,)), ((), ())), preferred_element_type=F32)


def tile_rows(index):
    return pl.ds(pl.multiple_of(index * TILE, TILE), TILE)


def rows_of(tile):
    return slice(tile * TILE, (tile + 1) * TILE)


def hot_rows(clus_row, first, count):
    ids = lax.broadcasted_iota(jnp.int32, (count, clus_row.shape[1]), 0) + first
    return jnp.where(ids == clus_row, 1.0, 0.0).astype(BF16)


def hot_columns(clus_row, clusters):
    spread = jnp.broadcast_to(clus_row.astype(F32), (TILE, TILE)).T
    spread = jnp.concatenate([spread] * (-(-clusters // TILE)), axis=1)[:, :clusters]
    ids = lax.broadcasted_iota(jnp.int32, (TILE, clusters), 1).astype(F32)
    return jnp.where(ids == spread, 1.0, 0.0).astype(BF16)


def slots(side):
    near, gy = lax.axis_index("core"), lax.rem(lax.axis_index("gy"), 2)
    out = (1 - near, 3 - gy, 2 + gy, near)
    return out if side == "out" else (near, 2 + gy, 3 - gy, 1 - near)


def call(kernel, outs, in_specs=None, scratch=(), limit=VMEM_LIMIT, out_specs=None, flops=0, moved=0):
    options = {}
    if in_specs is not None:
        options["in_specs"] = in_specs
    if out_specs is not None:
        options["out_specs"] = out_specs
    return pl.pallas_call(
        kernel,
        out_shape=outs,
        scratch_shapes=list(scratch),
        compiler_params=pltpu.CompilerParams(vmem_limit_bytes=limit),
        cost_estimate=pl.CostEstimate(flops=flops, bytes_accessed=moved, transcendentals=0),
        **options,
    )


def vmem(count):
    return [pl.BlockSpec(memory_space=pltpu.VMEM)] * count


def smem(count):
    return [pl.BlockSpec(memory_space=pltpu.SMEM)] * count


def like(shape, kind):
    return jax.ShapeDtypeStruct(shape, kind)


def fetch(far, near, sems):
    copies = [
        pltpu.make_async_copy(*pair, sems.at[index])
        for index, pair in enumerate(zip(far, near))
    ]
    for copy in copies:
        copy.start()
    return copies


def pool_kernel(share, clus_far, state_far, pool, clus, state, hot, sems):
    for copy in fetch((clus_far, state_far), (clus, state), sems):
        copy.wait()
    rows, features = state.shape
    clus_row = clus[...]
    line = lax.broadcasted_iota(jnp.int32, (16, TILE), 0)
    for peer in range(pool.shape[0]):
        hot[rows_of(peer)] = hot_rows(clus_row, peer * share, TILE)
    sums = mm(hot[...], state[...])
    counts = mm_nt(jnp.ones((16, rows), BF16), hot[...])
    for peer in range(pool.shape[0]):
        pool[peer, 0:share] = sums[peer * TILE:peer * TILE + share].astype(BF16)
        count = counts[:, rows_of(peer)]
        eights = jnp.floor(count * 0.125)
        high = jnp.floor(eights * 0.125)
        digits = jnp.where(
            line < 4, count - 8.0 * eights, jnp.where(line < 8, eights - 8.0 * high, high)
        )
        pool[peer, share:share + 16, 0:TILE] = digits.astype(BF16)
        pool[peer, share:share + 16, TILE:] = jnp.zeros((16, features - TILE), BF16)


def front_kernel(*refs):
    far, refs = refs[:10], refs[10:]
    (part0, part1, part2, part3, lifted, active, local, params), refs = refs[:8], refs[8:]
    near, (message, sems) = refs[:10], refs[10:]
    for copy in fetch(far, near, sems):
        copy.wait()
    (state, edge_bias, node_bias, norm_gain, edge_lift, edge_emit, source, adjacency, cuts,
     blocks) = near
    tiles = state.shape[0] // TILE
    params[...] = jnp.zeros(params.shape, F32)
    for index, vector in enumerate((node_bias, norm_gain)):
        params[index:index + 1] = vector[...].astype(F32).reshape(1, -1)
    bias = edge_bias[...].astype(F32).reshape(1, -1)
    value = (mm(state[...], edge_lift[...]) + bias).astype(BF16)
    lifted[...] = value
    wide = value.astype(F32)
    hidden = (wide * jax.nn.sigmoid(wide)).astype(BF16)
    active[...] = hidden
    message[...] = mm(hidden, edge_emit[...]).astype(BF16)
    for slot, part in zip(slots("out"), (part0, part1, part2, part3)):
        for cut in range(cuts.shape[1]):
            part[rows_of(cut)] = mm(
                cuts[slot, cut], message[tile_rows(source[cut, slot])]
            ).astype(BF16)
    for tile in range(tiles):
        total = mm(blocks[tile, 0], message[tile_rows(adjacency[tile, 0])])
        for slot in range(1, blocks.shape[1]):
            total += mm(blocks[tile, slot], message[tile_rows(adjacency[tile, slot])])
        local[rows_of(tile)] = total


def aggregate_kernel(target, _source, _adjacency, local, arrived0, arrived1, arrived2, arrived3,
                     aggregate, summed):
    summed[...] = local[...]
    for slot, arrived in zip(slots("in"), (arrived0, arrived1, arrived2, arrived3)):
        for cut in range(arrived.shape[0] // TILE):
            summed[tile_rows(target[cut, slot])] += arrived[rows_of(cut)].astype(F32)
    aggregate[...] = summed[...].astype(BF16)


def sum_kernel(received, out):
    out[...] = jnp.sum(received[...].astype(F32), axis=0).astype(BF16)


def add_kernel(mine, other, out):
    out[...] = (mine[...].astype(F32) + other[...].astype(F32)).astype(BF16)


def mean_kernel(share, mine, other, means, counts):
    total = mine[...].astype(F32) + other[...].astype(F32)
    low, middle, high = (total[share + row:share + row + 1, 0:TILE] for row in (0, 4, 8))
    count = jnp.broadcast_to(high * 64.0 + middle * 8.0 + low, (TILE, TILE)).T[:share]
    count = jnp.concatenate([count] * (means.shape[2] // TILE), axis=1)
    counts[...] = count
    mean = (total[:share] / count).astype(BF16)
    for peer in range(means.shape[0]):
        means[peer] = mean


def node_kernel(target, clus, state, upstream, aggregate, mine, other, node_lift, node_emit, params,
                updated, coarse, active, emit_grad, lifted_grad, aggregate_grad,
                coarse_grad, back0, back1, back2, back3, vectors, means, slopes, hot):
    features = state.shape[1]
    clusters, share = means.shape[0], mine.shape[1]
    core = lax.axis_index("core")
    for peer in range(clusters // share):
        means[peer * share:(peer + 1) * share] = jnp.where(
            core == peer % 2, mine[peer // 2], other[peer // 2]
        )
    lift_state = node_lift[0:features]
    lift_agg = node_lift[features:2 * features]
    lift_coarse = node_lift[2 * features:]
    bias = params[0:1]
    gain = params[1:2]
    gain_grad = jnp.zeros((1, features), F32)
    bias_grad = jnp.zeros((1, features), F32)
    here = state[...]
    for tile in range(state.shape[0] // TILE):
        hot[rows_of(tile)] = hot_columns(clus[0:1, rows_of(tile)], clusters)
    coarse[...] = mm(hot[...], means[...]).astype(BF16)
    lifted = (
        mm(here, lift_state) + mm(aggregate[...], lift_agg) + mm(coarse[...], lift_coarse)
        + bias
    ).astype(BF16).astype(F32)
    gate = jax.nn.sigmoid(lifted)
    hidden = (lifted * gate).astype(BF16)
    active[...] = hidden
    slopes[...] = gate * (1.0 + lifted * (1.0 - gate))
    emitted = mm(hidden, node_emit[...])
    center = emitted - jnp.mean(emitted, axis=-1, keepdims=True)
    inverse = lax.rsqrt(jnp.mean(center * center, axis=-1, keepdims=True) + NORM_EPS)
    normed = center * inverse
    updated[...] = (here.astype(F32) + gain * normed).astype(BF16)
    above = upstream[...].astype(F32)
    gain_grad += jnp.sum(above * normed, axis=0, keepdims=True)
    scaled = above * gain
    grad = (
        inverse
        * (
            scaled
            - jnp.mean(scaled, axis=-1, keepdims=True)
            - normed * jnp.mean(scaled * normed, axis=-1, keepdims=True)
        )
    ).astype(BF16)
    emit_grad[...] = grad
    active_grad = mm_nt(grad, node_emit[...]).astype(BF16).astype(F32)
    down = (active_grad * slopes[...]).astype(BF16)
    lifted_grad[...] = down
    bias_grad += jnp.sum(down.astype(F32), axis=0, keepdims=True)
    aggregate_grad[...] = mm_nt(down, lift_agg).astype(BF16)
    coarse_grad[...] = mm_nt(down, lift_coarse).astype(BF16)
    for slot, back in zip(slots("in"), (back0, back1, back2, back3)):
        for cut in range(back.shape[0] // TILE):
            back[rows_of(cut)] = aggregate_grad[tile_rows(target[cut, slot])]
    vectors[...] = jnp.zeros(vectors.shape, F32)
    vectors[0:1] = bias_grad
    vectors[1:2] = gain_grad


def put_chunks(packed, first, size, start, value):
    done = 0
    while done < value.shape[0]:
        peer, offset = divmod(start + done, size)
        count = min(size - offset, value.shape[0] - done)
        packed[peer, first + offset:first + offset + count] = value[done:done + count].astype(BF16)
        done += count


def part_ways(stack, keep, send, first=0):
    core = lax.axis_index("core")
    for index in range(keep.shape[0]):
        rows = slice(first, first + stack.shape[1])
        keep[index, rows] = stack[2 * index + core]
        send[index, rows] = stack[2 * index + 1 - core]


def weight_kernel(sizes, adjacency, clus, state, upstream, aggregate, coarse, active, emit_grad,
                  lifted_grad, aggregate_grad, coarse_grad, blocks, node_lift,
                  keep, send, local, partial, stack, hot):
    peers, share, node_rows, _ = sizes
    features = state.shape[1]
    clus_row = clus[...]
    for peer in range(peers):
        hot[peer * share:(peer + 1) * share] = hot_rows(clus_row, peer * share, share)
    put_chunks(stack, 0, share, 0, mm(hot[...], coarse_grad[...]))
    down = lifted_grad[...]
    for index, block in enumerate((state, aggregate, coarse)):
        put_chunks(stack, share, node_rows, index * features, mm_tn(block[...], down))
    put_chunks(stack, share, node_rows, 3 * features, mm_tn(active[...], emit_grad[...]))
    part_ways(stack, keep, send)
    partial[...] = upstream[...].astype(F32) + mm_nt(down, node_lift[0:features])
    local[...] = jnp.zeros(local.shape, F32)
    for tile in range(state.shape[0] // TILE):
        rows = rows_of(tile)
        for slot in range(blocks.shape[1]):
            local[tile_rows(adjacency[tile, slot])] += mm_tn(
                blocks[tile, slot], aggregate_grad[rows]
            )


def edge_kernel(sizes, source, state, lifted, active, local, back0, back1, back2, back3, cuts,
                edge_lift, edge_emit, partial, vectors, keep_node, send_node,
                keep, send, partial_out, total, message_grad, lifted_grad, edge_part):
    peers, _, _, edge_rows = sizes
    features = state.shape[1]
    total[...] = local[...]
    for slot, back in zip(slots("out"), (back0, back1, back2, back3)):
        for cut in range(cuts.shape[1]):
            total[tile_rows(source[cut, slot])] += mm_tn(cuts[slot, cut], back[rows_of(cut)])
    grad = total[...].astype(BF16)
    message_grad[...] = grad
    active_grad = mm_nt(grad, edge_emit[...]).astype(BF16).astype(F32)
    wide = lifted[...].astype(F32)
    gate = jax.nn.sigmoid(wide)
    down = (active_grad * (gate * (1.0 + wide * (1.0 - gate)))).astype(BF16)
    lifted_grad[...] = down
    bias_grad = jnp.sum(down.astype(F32), axis=0, keepdims=True)
    partial_out[...] = partial[...] + mm_nt(down, edge_lift[...])
    put_chunks(edge_part, 0, edge_rows, 0, mm_tn(state[...], lifted_grad[...]))
    put_chunks(edge_part, 0, edge_rows, features, mm_tn(active[...], message_grad[...]))
    edge_part[:, edge_rows:] = jnp.zeros((peers, 16, features), BF16)
    last = lax.broadcasted_iota(jnp.int32, (16, features), 0)
    edge_part[0, edge_rows:] = jnp.where(
        last == 0, vectors[0:1], jnp.where(last == 1, vectors[1:2], jnp.where(last == 2, bias_grad, 0.0))
    ).astype(BF16)
    part_ways(edge_part, keep, send, keep_node.shape[1])
    keep[:, 0:keep_node.shape[1]] = keep_node[...]
    send[:, 0:keep_node.shape[1]] = send_node[...]


def split_kernel(share, received, pool, grads):
    total = jnp.sum(received[...].astype(F32), axis=0).astype(BF16)
    pool[...] = total[:share]
    chunk = grads.shape[1]
    row = 0
    while row < total.shape[0] - share:
        index, offset = divmod(row, chunk)
        grads[index, offset:offset + 16] = total[share + row:share + row + 16]
        row += 16
    while row < grads.shape[0] * chunk:
        index, offset = divmod(row, chunk)
        grads[index, offset:offset + 16] = jnp.zeros((16, grads.shape[2]), BF16)
        row += 16


def join_kernel(pool, received, out):
    share = pool.shape[0]
    grads = jnp.sum(received[...].astype(F32), axis=0).astype(BF16)
    for peer in range(out.shape[0]):
        out[peer, 0:share] = pool[...]
        out[peer, share:] = grads


def settle_kernel(share, received, counts, means, grads):
    total = jnp.sum(received[...].astype(F32), axis=0)
    means[...] = (total[:share] / counts[...]).astype(BF16)
    whole = total[share:].astype(BF16)
    for index in range(grads.shape[0]):
        grads[index] = whole


def spread_kernel(means, grads, out):
    share, used = means.shape[0], out.shape[1] - means.shape[0]
    chunk = grads.shape[1]
    for peer in range(out.shape[0]):
        out[peer, 0:share] = means[...]
        for first in range(0, used, chunk):
            count = min(chunk, used - first)
            out[peer, share + first:share + first + count] = grads[first // chunk, 0:count]


def last_kernel(sizes, scale, clus, partial, mine, other, state_grad, edge_lift, edge_bias,
                edge_emit, node_lift, node_bias, node_emit, norm_gain, means, hot):
    peers, share, node_rows, edge_rows = sizes
    features = partial.shape[1]
    core = lax.axis_index("core")

    def gathered(peer, first, count):
        rows = slice(first, first + count)
        return jnp.where(core == peer % 2, mine[peer // 2, rows], other[peer // 2, rows])

    for peer in range(peers):
        means[peer * share:(peer + 1) * share] = gathered(peer, 0, share)
    for tile in range(partial.shape[0] // TILE):
        rows = rows_of(tile)
        hot[rows] = hot_columns(clus[0:1, rows], peers * share)
    state_grad[...] = (partial[...] + mm(hot[...], means[...])).astype(BF16)

    def take(first, size, outs):
        start = 0
        for out in outs:
            done = 0
            while done < out.shape[0]:
                peer, offset = divmod(start + done, size)
                count = min(size - offset, out.shape[0] - done)
                out[done:done + count] = gathered(peer, first + offset, count).astype(F32) * scale
                done += count
            start += done

    take(share, node_rows, (node_lift, node_emit))
    take(share + node_rows, edge_rows, (edge_lift, edge_emit))
    tail = gathered(0, share + node_rows + edge_rows, 16).astype(F32) * scale
    node_bias[...] = tail[0:1]
    norm_gain[...] = tail[1:2]
    edge_bias[...] = tail[2:3]


def shards(
    node_state,
    node_grad,
    edge_blocks,
    adjacency,
    cut_source,
    cut_target,
    cut_blocks,
    clusters,
    edge_lift,
    edge_bias,
    edge_emit,
    node_lift,
    node_bias,
    node_emit,
    norm_gain,
):
    near = ("y", "core")
    far, across, columns = (lax.axis_size(name) for name in ("far", "y", "gy"))
    peers = 2 * across
    rows, features = node_state.shape
    along = far * peers
    share = CLUS_DEV * far
    node_rows = 4 * features // peers
    edge_rows = 2 * features // peers
    sizes = (peers, share, node_rows, edge_rows)
    packed_rows = share + node_rows + edge_rows + 16
    chunk = -(-(packed_rows - share) // (16 * columns)) * 16
    source, target = cut_source[0, 0].T, cut_target[0, 0].T
    cuts = cut_blocks[0, 0]
    cut_rows = cuts.shape[1] * TILE
    clus = clusters.reshape(1, rows)
    wide = like((rows, features), F32)
    narrow = like((rows, features), BF16)
    cut_part = like((cut_rows, features), BF16)
    layer = 2 * rows * features * features

    gx = ("far", *near)
    both_cores = [(0, 1), (1, 0)]

    ways = ((gx, along, 1), ("gy", columns, 1), ("gy", columns, 0), (gx, along, 0))

    def swap(parts, ways=ways):
        moved = []
        for part, (axis, count, first) in zip(parts, ways):
            pairs = [(i, i + 1) for i in range(first, count - 1, 2)]
            moved.append(lax.ppermute(part, axis, pairs + [(j, i) for i, j in pairs]))
        return moved

    anywhere = pl.BlockSpec(memory_space=pl.ANY)
    pool = call(
        functools.partial(pool_kernel, share),
        like((peers, share + 16, features), BF16),
        [anywhere] * 2,
        [
            pltpu.VMEM((1, rows), jnp.int32),
            pltpu.VMEM((rows, features), BF16),
            pltpu.VMEM((peers * TILE, rows), BF16),
            pltpu.SemaphoreType.DMA((2,)),
        ],
        FIRST_LIMIT,
        out_specs=pl.BlockSpec(memory_space=pltpu.VMEM),
        flops=2 * layer,
        moved=1 << 20,
    )(clus, node_state)
    operands = (node_state, edge_bias, node_bias, norm_gain, edge_lift, edge_emit, source,
                adjacency, cuts, edge_blocks)
    tables = (source, adjacency)
    part0, part1, part2, part3, lifted, active, local, params = call(
        front_kernel,
        [cut_part] * 4 + [narrow, narrow, wide, like((8, features), F32)],
        [anywhere] * len(operands),
        [
            (pltpu.SMEM if any(v is table for table in tables) else pltpu.VMEM)(v.shape, v.dtype)
            for v in operands
        ]
        + [pltpu.VMEM((rows, features), BF16), pltpu.SemaphoreType.DMA((len(operands),))],
        FIRST_LIMIT,
        out_specs=vmem(8),
        flops=8 * layer,
        moved=4 << 20,
    )(*operands)
    received = lax.all_to_all(pool, near, 0, 0, tiled=True)
    summed = call(
        sum_kernel,
        like((share + 16, features), BF16),
        vmem(1),
        out_specs=pl.BlockSpec(memory_space=pltpu.VMEM),
        moved=1 << 20,
    )(received)
    meetings = [[(i, i ^ 1) for i in range(far)], [(i, far - 1 - i) for i in range(far)]]
    summed, part0, part1 = lax.optimization_barrier((summed, part0, part1))
    other = lax.ppermute(summed, "far", meetings[0])
    arrived = swap((part0, part1), ways[:2])
    if far > 2:
        summed = call(add_kernel, like(summed.shape, BF16), vmem(2), moved=1 << 18)(summed, other)
        summed, part2, part3 = lax.optimization_barrier((summed, part2, part3))
        other = lax.ppermute(summed, "far", meetings[1])
    arrived += swap((part2, part3), ways[2:])
    summed, other, *arrived = lax.optimization_barrier((summed, other, *arrived))
    means, counts = call(
        functools.partial(mean_kernel, share),
        [like((across, share, features), BF16), like((share, features), F32)],
        vmem(2),
        out_specs=vmem(2),
        moved=1 << 20,
    )(summed, other)
    my_means = lax.all_to_all(means, "y", 0, 0, tiled=True)
    other_means = lax.ppermute(my_means, "core", both_cores)
    local, my_means, *arrived = lax.optimization_barrier((local, my_means, *arrived))
    aggregate = call(
        aggregate_kernel,
        narrow,
        smem(3) + vmem(5),
        [pltpu.VMEM((rows, features), F32)],
        moved=2 << 20,
    )(target, source, adjacency, local, *arrived)

    (updated, coarse, node_active, emit_grad, lifted_grad, aggregate_grad, coarse_grad,
     back0, back1, back2, back3, vectors) = call(
        node_kernel,
        [narrow] * 7 + [cut_part] * 4 + [like((8, features), F32)],
        smem(1) + vmem(9),
        [
            pltpu.VMEM((peers * share, features), BF16),
            pltpu.VMEM((rows, features), F32),
            pltpu.VMEM((rows, peers * share), BF16),
        ],
        flops=10 * layer,
        moved=4 << 20,
    )(target, clus, node_state, node_grad, aggregate, my_means, other_means, node_lift, node_emit,
      params)

    keep_node, send_node, message_local, partial = call(
        functools.partial(weight_kernel, sizes),
        [like((across, share + node_rows, features), BF16)] * 2 + [wide, wide],
        smem(1) + vmem(12),
        [
            pltpu.VMEM((peers, share + node_rows, features), BF16),
            pltpu.VMEM((peers * share, rows), BF16),
        ],
        flops=8 * layer,
        moved=5 << 20,
    )(adjacency, clus, node_state, node_grad, aggregate, coarse, node_active, emit_grad,
      lifted_grad, aggregate_grad, coarse_grad, edge_blocks, node_lift)
    returned = swap((back0, back1, back2, back3))
    keep, send, partial = call(
        functools.partial(edge_kernel, sizes),
        [like((across, packed_rows, features), BF16)] * 2 + [wide],
        smem(1) + vmem(15),
        [
            pltpu.VMEM((rows, features), F32),
            pltpu.VMEM((rows, features), BF16),
            pltpu.VMEM((rows, features), BF16),
            pltpu.VMEM((peers, edge_rows + 16, features), BF16),
        ],
        flops=8 * layer,
        moved=5 << 20,
    )(source, node_state, lifted, active, message_local, *returned, cuts, edge_lift, edge_emit,
      partial, vectors, keep_node, send_node)
    got = lax.ppermute(send, "core", both_cores)
    merged = call(add_kernel, like(keep.shape, BF16), vmem(2), moved=2 << 20)(keep, got)
    received = lax.all_to_all(merged, "y", 0, 0, tiled=True)
    pool, grads = call(
        functools.partial(split_kernel, share),
        [like((share, features), BF16), like((columns, chunk, features), BF16)],
        vmem(1),
        moved=1 << 20,
    )(received)
    received = lax.all_to_all(grads, "gy", 0, 0, tiled=True)
    joined = call(
        join_kernel, like((far, share + chunk, features), BF16), vmem(2), moved=1 << 20
    )(pool, received)
    received = lax.all_to_all(joined, "far", 0, 0, tiled=True)
    means, grads = call(
        functools.partial(settle_kernel, share),
        [like((share, features), BF16), like((columns, chunk, features), BF16)],
        vmem(2),
        moved=1 << 20,
    )(received, counts)
    grads = lax.all_to_all(grads, "gy", 0, 0, tiled=True)
    spread = call(
        spread_kernel, like((across, packed_rows, features), BF16), vmem(2), moved=2 << 20
    )(means, grads)
    mine = lax.all_to_all(spread, "y", 0, 0, tiled=True)
    other = lax.ppermute(mine, "core", both_cores)
    scale = float(rows * along * columns) ** (-0.5)
    square, line = like((features, features), F32), like((1, features), F32)
    (state_grad, edge_lift_grad, edge_bias_grad, edge_emit_grad, node_lift_grad, node_bias_grad,
     node_emit_grad, gain_grad) = call(
        functools.partial(last_kernel, sizes, scale),
        [narrow, square, line, square, like((3 * features, features), F32), line, square, line],
        vmem(4),
        [pltpu.VMEM((peers * share, features), BF16), pltpu.VMEM((rows, peers * share), BF16)],
        flops=3 * layer,
        moved=4 << 20,
    )(clus, partial, mine, other)
    return (
        updated,
        state_grad,
        edge_lift_grad,
        edge_bias_grad.reshape(features),
        edge_emit_grad,
        node_lift_grad,
        node_bias_grad.reshape(features),
        node_emit_grad,
        gain_grad.reshape(features),
    )


def solution(mesh):
    gx, gy = mesh.shape["gx"], mesh.shape["gy"]
    near = 8 if gx % 8 == 0 and gx > 8 else 4
    grid = Mesh(
        mesh.devices.reshape(gx // near, near // 2, 2, gy), ("far", "y", "core", "gy")
    )
    across = ("far", "y", "core")
    both = (*across, "gy")
    placed = (
        P(both, None),
        P(both, None),
        P(both, None, None, None),
        P(both, None),
        P(across, "gy", None, None),
        P(across, "gy", None, None),
        P(across, "gy", None, None, None, None),
        P(both),
        P(),
        P(),
        P(),
        P(),
        P(),
        P(),
        P(),
    )
    return jax.shard_map(
        shards,
        mesh=grid,
        in_specs=placed,
        out_specs=(P(both, None), P(both, None), P(), P(), P(), P(), P(), P(), P()),
        check_vma=False,
    )
```

```python
import functools

import jax
import jax.numpy as jnp
from jax import lax
from jax.experimental import pallas as pl
from jax.experimental.pallas import tpu as pltpu
from jax.sharding import Mesh
from jax.sharding import PartitionSpec as P

CLUS_DEV = 24
NORM_EPS = 1e-05
TILE = 128
F32 = jnp.float32
BF16 = jnp.bfloat16
VMEM_LIMIT = 24 * 1024 * 1024
FIRST_LIMIT = 60 * 1024 * 1024


def mm(left, right):
    return jnp.dot(left, right, preferred_element_type=F32)


def mm_tn(left, right):
    return lax.dot_general(left, right, (((0,), (0,)), ((), ())), preferred_element_type=F32)


def mm_nt(left, right):
    return lax.dot_general(left, right, (((1,), (1,)), ((), ())), preferred_element_type=F32)


def tile_rows(index):
    return pl.ds(pl.multiple_of(index * TILE, TILE), TILE)


def rows_of(tile):
    return slice(tile * TILE, (tile + 1) * TILE)


def hot_rows(clus_row, first, count):
    ids = lax.broadcasted_iota(jnp.int32, (count, clus_row.shape[1]), 0) + first
    return jnp.where(ids == clus_row, 1.0, 0.0).astype(BF16)


def hot_columns(clus_row, clusters):
    spread = jnp.broadcast_to(clus_row.astype(F32), (TILE, TILE)).T
    spread = jnp.concatenate([spread] * (-(-clusters // TILE)), axis=1)[:, :clusters]
    ids = lax.broadcasted_iota(jnp.int32, (TILE, clusters), 1).astype(F32)
    return jnp.where(ids == spread, 1.0, 0.0).astype(BF16)


def slots(side):
    near, gy = lax.axis_index("core"), lax.rem(lax.axis_index("gy"), 2)
    out = (1 - near, 3 - gy, 2 + gy, near)
    return out if side == "out" else (near, 2 + gy, 3 - gy, 1 - near)


def call(kernel, outs, in_specs=None, scratch=(), limit=VMEM_LIMIT, out_specs=None, flops=0, moved=0):
    options = {}
    if in_specs is not None:
        options["in_specs"] = in_specs
    if out_specs is not None:
        options["out_specs"] = out_specs
    return pl.pallas_call(
        kernel,
        out_shape=outs,
        scratch_shapes=list(scratch),
        compiler_params=pltpu.CompilerParams(vmem_limit_bytes=limit),
        cost_estimate=pl.CostEstimate(flops=flops, bytes_accessed=moved, transcendentals=0),
        **options,
    )


def vmem(count):
    return [pl.BlockSpec(memory_space=pltpu.VMEM)] * count


def smem(count):
    return [pl.BlockSpec(memory_space=pltpu.SMEM)] * count


def like(shape, kind):
    return jax.ShapeDtypeStruct(shape, kind)


def fetch(far, near, sems):
    copies = [
        pltpu.make_async_copy(*pair, sems.at[index])
        for index, pair in enumerate(zip(far, near))
    ]
    for copy in copies:
        copy.start()
    return copies


def pool_kernel(share, clus_far, state_far, pool, clus, state, hot, sems):
    for copy in fetch((clus_far, state_far), (clus, state), sems):
        copy.wait()
    rows, features = state.shape
    clus_row = clus[...]
    line = lax.broadcasted_iota(jnp.int32, (16, TILE), 0)
    for peer in range(pool.shape[0]):
        hot[rows_of(peer)] = hot_rows(clus_row, peer * share, TILE)
    sums = mm(hot[...], state[...])
    counts = mm_nt(jnp.ones((16, rows), BF16), hot[...])
    for peer in range(pool.shape[0]):
        pool[peer, 0:share] = sums[peer * TILE:peer * TILE + share].astype(BF16)
        count = counts[:, rows_of(peer)]
        eights = jnp.floor(count * 0.125)
        high = jnp.floor(eights * 0.125)
        digits = jnp.where(
            line < 4, count - 8.0 * eights, jnp.where(line < 8, eights - 8.0 * high, high)
        )
        pool[peer, share:share + 16, 0:TILE] = digits.astype(BF16)
        pool[peer, share:share + 16, TILE:] = jnp.zeros((16, features - TILE), BF16)


def front_kernel(*refs):
    far, refs = refs[:10], refs[10:]
    (part0, part1, part2, part3, lifted, active, local, params), refs = refs[:8], refs[8:]
    near, (message, sems) = refs[:10], refs[10:]
    for copy in fetch(far, near, sems):
        copy.wait()
    (state, edge_bias, node_bias, norm_gain, edge_lift, edge_emit, source, adjacency, cuts,
     blocks) = near
    tiles = state.shape[0] // TILE
    params[...] = jnp.zeros(params.shape, F32)
    for index, vector in enumerate((node_bias, norm_gain)):
        params[index:index + 1] = vector[...].astype(F32).reshape(1, -1)
    bias = edge_bias[...].astype(F32).reshape(1, -1)
    value = (mm(state[...], edge_lift[...]) + bias).astype(BF16)
    lifted[...] = value
    wide = value.astype(F32)
    hidden = (wide * jax.nn.sigmoid(wide)).astype(BF16)
    active[...] = hidden
    message[...] = mm(hidden, edge_emit[...]).astype(BF16)
    for slot, part in zip(slots("out"), (part0, part1, part2, part3)):
        for cut in range(cuts.shape[1]):
            part[rows_of(cut)] = mm(
                cuts[slot, cut], message[tile_rows(source[cut, slot])]
            ).astype(BF16)
    for tile in range(tiles):
        total = mm(blocks[tile, 0], message[tile_rows(adjacency[tile, 0])])
        for slot in range(1, blocks.shape[1]):
            total += mm(blocks[tile, slot], message[tile_rows(adjacency[tile, slot])])
        local[rows_of(tile)] = total


def aggregate_kernel(target, _source, _adjacency, local, arrived0, arrived1, arrived2, arrived3,
                     aggregate, summed):
    summed[...] = local[...]
    for slot, arrived in zip(slots("in"), (arrived0, arrived1, arrived2, arrived3)):
        for cut in range(arrived.shape[0] // TILE):
            summed[tile_rows(target[cut, slot])] += arrived[rows_of(cut)].astype(F32)
    aggregate[...] = summed[...].astype(BF16)


def sum_kernel(received, out):
    out[...] = jnp.sum(received[...].astype(F32), axis=0).astype(BF16)


def add_kernel(mine, other, out):
    out[...] = (mine[...].astype(F32) + other[...].astype(F32)).astype(BF16)


def mean_kernel(share, mine, other, means, counts):
    total = mine[...].astype(F32) + other[...].astype(F32)
    low, middle, high = (total[share + row:share + row + 1, 0:TILE] for row in (0, 4, 8))
    count = jnp.broadcast_to(high * 64.0 + middle * 8.0 + low, (TILE, TILE)).T[:share]
    count = jnp.concatenate([count] * (means.shape[2] // TILE), axis=1)
    counts[...] = count
    mean = (total[:share] / count).astype(BF16)
    for peer in range(means.shape[0]):
        means[peer] = mean


def node_kernel(target, clus, state, upstream, aggregate, mine, other, node_lift, node_emit, params,
                updated, coarse, active, emit_grad, lifted_grad, aggregate_grad,
                coarse_grad, back0, back1, back2, back3, vectors, means, slopes, hot):
    features = state.shape[1]
    clusters, share = means.shape[0], mine.shape[1]
    core = lax.axis_index("core")
    for peer in range(clusters // share):
        means[peer * share:(peer + 1) * share] = jnp.where(
            core == peer % 2, mine[peer // 2], other[peer // 2]
        )
    lift_state = node_lift[0:features]
    lift_agg = node_lift[features:2 * features]
    lift_coarse = node_lift[2 * features:]
    bias = params[0:1]
    gain = params[1:2]
    gain_grad = jnp.zeros((1, features), F32)
    bias_grad = jnp.zeros((1, features), F32)
    here = state[...]
    for tile in range(state.shape[0] // TILE):
        hot[rows_of(tile)] = hot_columns(clus[0:1, rows_of(tile)], clusters)
    coarse[...] = mm(hot[...], means[...]).astype(BF16)
    lifted = (
        mm(here, lift_state) + mm(aggregate[...], lift_agg) + mm(coarse[...], lift_coarse)
        + bias
    ).astype(BF16).astype(F32)
    gate = jax.nn.sigmoid(lifted)
    hidden = (lifted * gate).astype(BF16)
    active[...] = hidden
    slopes[...] = gate * (1.0 + lifted * (1.0 - gate))
    emitted = mm(hidden, node_emit[...])
    center = emitted - jnp.mean(emitted, axis=-1, keepdims=True)
    inverse = lax.rsqrt(jnp.mean(center * center, axis=-1, keepdims=True) + NORM_EPS)
    normed = center * inverse
    updated[...] = (here.astype(F32) + gain * normed).astype(BF16)
    above = upstream[...].astype(F32)
    gain_grad += jnp.sum(above * normed, axis=0, keepdims=True)
    scaled = above * gain
    grad = (
        inverse
        * (
            scaled
            - jnp.mean(scaled, axis=-1, keepdims=True)
            - normed * jnp.mean(scaled * normed, axis=-1, keepdims=True)
        )
    ).astype(BF16)
    emit_grad[...] = grad
    active_grad = mm_nt(grad, node_emit[...]).astype(BF16).astype(F32)
    down = (active_grad * slopes[...]).astype(BF16)
    lifted_grad[...] = down
    bias_grad += jnp.sum(down.astype(F32), axis=0, keepdims=True)
    aggregate_grad[...] = mm_nt(down, lift_agg).astype(BF16)
    coarse_grad[...] = mm_nt(down, lift_coarse).astype(BF16)
    for slot, back in zip(slots("in"), (back0, back1, back2, back3)):
        for cut in range(back.shape[0] // TILE):
            back[rows_of(cut)] = aggregate_grad[tile_rows(target[cut, slot])]
    vectors[...] = jnp.zeros(vectors.shape, F32)
    vectors[0:1] = bias_grad
    vectors[1:2] = gain_grad


def put_chunks(packed, first, size, start, value):
    done = 0
    while done < value.shape[0]:
        peer, offset = divmod(start + done, size)
        count = min(size - offset, value.shape[0] - done)
        packed[peer, first + offset:first + offset + count] = value[done:done + count].astype(BF16)
        done += count


def part_ways(stack, keep, send, first=0):
    core = lax.axis_index("core")
    for index in range(keep.shape[0]):
        rows = slice(first, first + stack.shape[1])
        keep[index, rows] = stack[2 * index + core]
        send[index, rows] = stack[2 * index + 1 - core]


def weight_kernel(sizes, adjacency, clus, state, upstream, aggregate, coarse, active, emit_grad,
                  lifted_grad, aggregate_grad, coarse_grad, blocks, node_lift,
                  keep, send, local, partial, stack, hot):
    peers, share, node_rows, _ = sizes
    features = state.shape[1]
    clus_row = clus[...]
    for peer in range(peers):
        hot[peer * share:(peer + 1) * share] = hot_rows(clus_row, peer * share, share)
    put_chunks(stack, 0, share, 0, mm(hot[...], coarse_grad[...]))
    down = lifted_grad[...]
    for index, block in enumerate((state, aggregate, coarse)):
        put_chunks(stack, share, node_rows, index * features, mm_tn(block[...], down))
    put_chunks(stack, share, node_rows, 3 * features, mm_tn(active[...], emit_grad[...]))
    part_ways(stack, keep, send)
    partial[...] = upstream[...].astype(F32) + mm_nt(down, node_lift[0:features])
    local[...] = jnp.zeros(local.shape, F32)
    for tile in range(state.shape[0] // TILE):
        rows = rows_of(tile)
        for slot in range(blocks.shape[1]):
            local[tile_rows(adjacency[tile, slot])] += mm_tn(
                blocks[tile, slot], aggregate_grad[rows]
            )


def edge_kernel(sizes, source, state, lifted, active, local, back0, back1, back2, back3, cuts,
                edge_lift, edge_emit, partial, vectors, keep_node, send_node,
                keep, send, partial_out, total, message_grad, lifted_grad, edge_part):
    peers, _, _, edge_rows = sizes
    features = state.shape[1]
    total[...] = local[...]
    for slot, back in zip(slots("out"), (back0, back1, back2, back3)):
        for cut in range(cuts.shape[1]):
            total[tile_rows(source[cut, slot])] += mm_tn(cuts[slot, cut], back[rows_of(cut)])
    grad = total[...].astype(BF16)
    message_grad[...] = grad
    active_grad = mm_nt(grad, edge_emit[...]).astype(BF16).astype(F32)
    wide = lifted[...].astype(F32)
    gate = jax.nn.sigmoid(wide)
    down = (active_grad * (gate * (1.0 + wide * (1.0 - gate)))).astype(BF16)
    lifted_grad[...] = down
    bias_grad = jnp.sum(down.astype(F32), axis=0, keepdims=True)
    partial_out[...] = partial[...] + mm_nt(down, edge_lift[...])
    put_chunks(edge_part, 0, edge_rows, 0, mm_tn(state[...], lifted_grad[...]))
    put_chunks(edge_part, 0, edge_rows, features, mm_tn(active[...], message_grad[...]))
    edge_part[:, edge_rows:] = jnp.zeros((peers, 16, features), BF16)
    last = lax.broadcasted_iota(jnp.int32, (16, features), 0)
    edge_part[0, edge_rows:] = jnp.where(
        last == 0, vectors[0:1], jnp.where(last == 1, vectors[1:2], jnp.where(last == 2, bias_grad, 0.0))
    ).astype(BF16)
    part_ways(edge_part, keep, send, keep_node.shape[1])
    keep[:, 0:keep_node.shape[1]] = keep_node[...]
    send[:, 0:keep_node.shape[1]] = send_node[...]


def split_kernel(share, received, pool, grads):
    total = jnp.sum(received[...].astype(F32), axis=0).astype(BF16)
    pool[...] = total[:share]
    chunk = grads.shape[1]
    row = 0
    while row < total.shape[0] - share:
        index, offset = divmod(row, chunk)
        grads[index, offset:offset + 16] = total[share + row:share + row + 16]
        row += 16
    while row < grads.shape[0] * chunk:
        index, offset = divmod(row, chunk)
        grads[index, offset:offset + 16] = jnp.zeros((16, grads.shape[2]), BF16)
        row += 16


def join_kernel(pool, received, out):
    share = pool.shape[0]
    grads = jnp.sum(received[...].astype(F32), axis=0).astype(BF16)
    for peer in range(out.shape[0]):
        out[peer, 0:share] = pool[...]
        out[peer, share:] = grads


def settle_kernel(share, received, counts, means, grads):
    total = jnp.sum(received[...].astype(F32), axis=0)
    means[...] = (total[:share] / counts[...]).astype(BF16)
    whole = total[share:].astype(BF16)
    for index in range(grads.shape[0]):
        grads[index] = whole


def spread_kernel(means, grads, out):
    share, used = means.shape[0], out.shape[1] - means.shape[0]
    chunk = grads.shape[1]
    for peer in range(out.shape[0]):
        out[peer, 0:share] = means[...]
        for first in range(0, used, chunk):
            count = min(chunk, used - first)
            out[peer, share + first:share + first + count] = grads[first // chunk, 0:count]


def pooled_kernel(share, clus, partial, mine, hot, out, means):
    core = lax.axis_index("core")
    peers = means.shape[0] // share
    for peer in range(peers):
        chunk = mine[peer // 2, 0:share]
        means[peer * share:(peer + 1) * share] = jnp.where(
            core == peer % 2, chunk, jnp.zeros_like(chunk)
        )
    for tile in range(partial.shape[0] // TILE):
        rows = rows_of(tile)
        hot[rows] = hot_columns(clus[0:1, rows], peers * share)
    out[...] = partial[...] + mm(hot[...], means[...])


def last_kernel(sizes, scale, hot, partial, mine, other, state_grad, edge_lift, edge_bias,
                edge_emit, node_lift, node_bias, node_emit, norm_gain, means):
    peers, share, node_rows, edge_rows = sizes
    features = partial.shape[1]
    core = lax.axis_index("core")

    def gathered(peer, first, count):
        rows = slice(first, first + count)
        return jnp.where(core == peer % 2, mine[peer // 2, rows], other[peer // 2, rows])

    for peer in range(peers):
        chunk = other[peer // 2, 0:share]
        means[peer * share:(peer + 1) * share] = jnp.where(
            core == peer % 2, jnp.zeros_like(chunk), chunk
        )
    state_grad[...] = (partial[...] + mm(hot[...], means[...])).astype(BF16)

    def take(first, size, outs):
        start = 0
        for out in outs:
            done = 0
            while done < out.shape[0]:
                peer, offset = divmod(start + done, size)
                count = min(size - offset, out.shape[0] - done)
                out[done:done + count] = gathered(peer, first + offset, count).astype(F32) * scale
                done += count
            start += done

    take(share, node_rows, (node_lift, node_emit))
    take(share + node_rows, edge_rows, (edge_lift, edge_emit))
    tail = gathered(0, share + node_rows + edge_rows, 16).astype(F32) * scale
    node_bias[...] = tail[0:1]
    norm_gain[...] = tail[1:2]
    edge_bias[...] = tail[2:3]


def shards(
    node_state,
    node_grad,
    edge_blocks,
    adjacency,
    cut_source,
    cut_target,
    cut_blocks,
    clusters,
    edge_lift,
    edge_bias,
    edge_emit,
    node_lift,
    node_bias,
    node_emit,
    norm_gain,
):
    near = ("y", "core")
    far, across, columns = (lax.axis_size(name) for name in ("far", "y", "gy"))
    peers = 2 * across
    rows, features = node_state.shape
    along = far * peers
    share = CLUS_DEV * far
    node_rows = 4 * features // peers
    edge_rows = 2 * features // peers
    sizes = (peers, share, node_rows, edge_rows)
    packed_rows = share + node_rows + edge_rows + 16
    chunk = -(-(packed_rows - share) // (16 * columns)) * 16
    source, target = cut_source[0, 0].T, cut_target[0, 0].T
    cuts = cut_blocks[0, 0]
    cut_rows = cuts.shape[1] * TILE
    clus = clusters.reshape(1, rows)
    wide = like((rows, features), F32)
    narrow = like((rows, features), BF16)
    cut_part = like((cut_rows, features), BF16)
    layer = 2 * rows * features * features

    gx = ("far", *near)
    both_cores = [(0, 1), (1, 0)]

    ways = ((gx, along, 1), ("gy", columns, 1), ("gy", columns, 0), (gx, along, 0))

    def swap(parts, ways=ways):
        moved = []
        for part, (axis, count, first) in zip(parts, ways):
            pairs = [(i, i + 1) for i in range(first, count - 1, 2)]
            moved.append(lax.ppermute(part, axis, pairs + [(j, i) for i, j in pairs]))
        return moved

    anywhere = pl.BlockSpec(memory_space=pl.ANY)
    pool = call(
        functools.partial(pool_kernel, share),
        like((peers, share + 16, features), BF16),
        [anywhere] * 2,
        [
            pltpu.VMEM((1, rows), jnp.int32),
            pltpu.VMEM((rows, features), BF16),
            pltpu.VMEM((peers * TILE, rows), BF16),
            pltpu.SemaphoreType.DMA((2,)),
        ],
        FIRST_LIMIT,
        out_specs=pl.BlockSpec(memory_space=pltpu.VMEM),
        flops=2 * layer,
        moved=1 << 20,
    )(clus, node_state)
    operands = (node_state, edge_bias, node_bias, norm_gain, edge_lift, edge_emit, source,
                adjacency, cuts, edge_blocks)
    tables = (source, adjacency)
    part0, part1, part2, part3, lifted, active, local, params = call(
        front_kernel,
        [cut_part] * 4 + [narrow, narrow, wide, like((8, features), F32)],
        [anywhere] * len(operands),
        [
            (pltpu.SMEM if any(v is table for table in tables) else pltpu.VMEM)(v.shape, v.dtype)
            for v in operands
        ]
        + [pltpu.VMEM((rows, features), BF16), pltpu.SemaphoreType.DMA((len(operands),))],
        FIRST_LIMIT,
        out_specs=vmem(8),
        flops=8 * layer,
        moved=4 << 20,
    )(*operands)
    received = lax.all_to_all(pool, near, 0, 0, tiled=True)
    summed = call(
        sum_kernel,
        like((share + 16, features), BF16),
        vmem(1),
        out_specs=pl.BlockSpec(memory_space=pltpu.VMEM),
        moved=1 << 20,
    )(received)
    meetings = [[(i, i ^ 1) for i in range(far)], [(i, far - 1 - i) for i in range(far)]]
    summed, part0, part1 = lax.optimization_barrier((summed, part0, part1))
    other = lax.ppermute(summed, "far", meetings[0])
    arrived = swap((part0, part1), ways[:2])
    if far > 2:
        summed = call(add_kernel, like(summed.shape, BF16), vmem(2), moved=1 << 18)(summed, other)
        summed, part2, part3 = lax.optimization_barrier((summed, part2, part3))
        other = lax.ppermute(summed, "far", meetings[1])
    arrived += swap((part2, part3), ways[2:])
    summed, other, *arrived = lax.optimization_barrier((summed, other, *arrived))
    means, counts = call(
        functools.partial(mean_kernel, share),
        [like((across, share, features), BF16), like((share, features), F32)],
        vmem(2),
        out_specs=vmem(2),
        moved=1 << 20,
    )(summed, other)
    my_means = lax.all_to_all(means, "y", 0, 0, tiled=True)
    other_means = lax.ppermute(my_means, "core", both_cores)
    aggregate = call(
        aggregate_kernel,
        narrow,
        smem(3) + vmem(5),
        [pltpu.VMEM((rows, features), F32)],
        moved=2 << 20,
    )(target, source, adjacency, local, *arrived)

    (updated, coarse, node_active, emit_grad, lifted_grad, aggregate_grad, coarse_grad,
     back0, back1, back2, back3, vectors) = call(
        node_kernel,
        [narrow] * 7 + [cut_part] * 4 + [like((8, features), F32)],
        smem(1) + vmem(9),
        [
            pltpu.VMEM((peers * share, features), BF16),
            pltpu.VMEM((rows, features), F32),
            pltpu.VMEM((rows, peers * share), BF16),
        ],
        flops=10 * layer,
        moved=4 << 20,
    )(target, clus, node_state, node_grad, aggregate, my_means, other_means, node_lift, node_emit,
      params)

    keep_node, send_node, message_local, partial = call(
        functools.partial(weight_kernel, sizes),
        [like((across, share + node_rows, features), BF16)] * 2 + [wide, wide],
        smem(1) + vmem(12),
        [
            pltpu.VMEM((peers, share + node_rows, features), BF16),
            pltpu.VMEM((peers * share, rows), BF16),
        ],
        flops=8 * layer,
        moved=5 << 20,
    )(adjacency, clus, node_state, node_grad, aggregate, coarse, node_active, emit_grad,
      lifted_grad, aggregate_grad, coarse_grad, edge_blocks, node_lift)
    returned = swap((back0, back1, back2, back3))
    keep, send, partial = call(
        functools.partial(edge_kernel, sizes),
        [like((across, packed_rows, features), BF16)] * 2 + [wide],
        smem(1) + vmem(15),
        [
            pltpu.VMEM((rows, features), F32),
            pltpu.VMEM((rows, features), BF16),
            pltpu.VMEM((rows, features), BF16),
            pltpu.VMEM((peers, edge_rows + 16, features), BF16),
        ],
        flops=8 * layer,
        moved=5 << 20,
    )(source, node_state, lifted, active, message_local, *returned, cuts, edge_lift, edge_emit,
      partial, vectors, keep_node, send_node)
    got = lax.ppermute(send, "core", both_cores)
    merged = call(add_kernel, like(keep.shape, BF16), vmem(2), moved=2 << 20)(keep, got)
    received = lax.all_to_all(merged, "y", 0, 0, tiled=True)
    pool, grads = call(
        functools.partial(split_kernel, share),
        [like((share, features), BF16), like((columns, chunk, features), BF16)],
        vmem(1),
        moved=1 << 20,
    )(received)
    received = lax.all_to_all(grads, "gy", 0, 0, tiled=True)
    joined = call(
        join_kernel, like((far, share + chunk, features), BF16), vmem(2), moved=1 << 20
    )(pool, received)
    received = lax.all_to_all(joined, "far", 0, 0, tiled=True)
    means, grads = call(
        functools.partial(settle_kernel, share),
        [like((share, features), BF16), like((columns, chunk, features), BF16)],
        vmem(2),
        moved=1 << 20,
    )(received, counts)
    grads = lax.all_to_all(grads, "gy", 0, 0, tiled=True)
    spread = call(
        spread_kernel, like((across, packed_rows, features), BF16), vmem(2), moved=2 << 20
    )(means, grads)
    mine = lax.all_to_all(spread, "y", 0, 0, tiled=True)
    other = lax.ppermute(mine, "core", both_cores)
    hot, partial = call(
        functools.partial(pooled_kernel, share),
        [like((rows, peers * share), BF16), wide],
        vmem(3),
        [pltpu.VMEM((peers * share, features), BF16)],
        flops=3 * layer,
        moved=4 << 20,
    )(clus, partial, mine)
    scale = float(rows * along * columns) ** (-0.5)
    square, line = like((features, features), F32), like((1, features), F32)
    (state_grad, edge_lift_grad, edge_bias_grad, edge_emit_grad, node_lift_grad, node_bias_grad,
     node_emit_grad, gain_grad) = call(
        functools.partial(last_kernel, sizes, scale),
        [narrow, square, line, square, like((3 * features, features), F32), line, square, line],
        vmem(4),
        [pltpu.VMEM((peers * share, features), BF16)],
        flops=3 * layer,
        moved=4 << 20,
    )(hot, partial, mine, other)
    return (
        updated,
        state_grad,
        edge_lift_grad,
        edge_bias_grad.reshape(features),
        edge_emit_grad,
        node_lift_grad,
        node_bias_grad.reshape(features),
        node_emit_grad,
        gain_grad.reshape(features),
    )


def solution(mesh):
    gx, gy = mesh.shape["gx"], mesh.shape["gy"]
    near = 8 if gx % 8 == 0 and gx > 8 else 4
    grid = Mesh(
        mesh.devices.reshape(gx // near, near // 2, 2, gy), ("far", "y", "core", "gy")
    )
    across = ("far", "y", "core")
    both = (*across, "gy")
    placed = (
        P(both, None),
        P(both, None),
        P(both, None, None, None),
        P(both, None),
        P(across, "gy", None, None),
        P(across, "gy", None, None),
        P(across, "gy", None, None, None, None),
        P(both),
        P(),
        P(),
        P(),
        P(),
        P(),
        P(),
        P(),
    )
    return jax.shard_map(
        shards,
        mesh=grid,
        in_specs=placed,
        out_specs=(P(both, None), P(both, None), P(), P(), P(), P(), P(), P(), P()),
        check_vma=False,
    )
```
